128 devices in a mesh: dp: 16 (over z, x), tensor: 8 (over y, core).
Axes of the slice: x: 4, y: 4, z: 4, core: 2. Of those that a mesh axis runs over, the one named last changes fastest.
Arguments:
- inputs: bfloat16 [16, 512, 1536], P('dp'), may hold values from -6 to 6
- norm_weight: float32 [1536], replicated, may hold values from 0.5 to 1.5
- gate_proj: bfloat16 [1536, 3072], P(None, 'tensor'), may hold values from -0.15625 to 0.15625
- inner_proj: bfloat16 [1536, 3072], P(None, 'tensor'), may hold values from -0.15625 to 0.15625
- state_proj: bfloat16 [1536, 256], replicated, may hold values from -0.15625 to 0.15625
- step_proj: bfloat16 [1536, 48], P(None, 'tensor'), may hold values from -0.15625 to 0.15625
- inner_conv: float32 [4, 3072], P(None, 'tensor'), may hold values from -3 to 3
- inner_conv_bias: float32 [3072], P('tensor'), may hold values from -1.5 to 1.5
- state_conv: float32 [4, 256], replicated, may hold values from -3 to 3
- state_conv_bias: float32 [256], replicated, may hold values from -1.5 to 1.5
- step_bias: float32 [48], P('tensor'), may hold values from -6.9 to -2.25
- decay_log: float32 [48], P('tensor'), may hold values from 0 to 2.77
- skip_weight: float32 [48], P('tensor'), may hold values from 0.5 to 1.5
- gated_norm_weight: float32 [3072], P('tensor'), may hold values from 0.5 to 1.5
- out_proj: bfloat16 [3072, 1536], P('tensor'), may hold values from -0.109375 to 0.109375
- segments: int32 [16, 512], P('dp'), may hold values from 0 to 2, never falling along the last dimension, each value on 1 to 256 neighbouring positions
- cotangent: bfloat16 [16, 512, 1536], P('dp'), may hold values from -6 to 6
Outputs:
- outputs: bfloat16 [16, 512, 1536], P('dp')
- input_grad: float32 [16, 512, 1536], P('dp')
- norm_weight_grad: float32 [1536], replicated
- gate_proj_grad: float32 [1536, 3072], P(None, 'tensor')
- inner_proj_grad: float32 [1536, 3072], P(None, 'tensor')
- state_proj_grad: float32 [1536, 256], replicated
- step_proj_grad: float32 [1536, 48], P(None, 'tensor')
- inner_conv_grad: float32 [4, 3072], P(None, 'tensor')
- inner_conv_bias_grad: float32 [3072], P('tensor')
- state_conv_grad: float32 [4, 256], replicated
- state_conv_bias_grad: float32 [256], replicated
- step_bias_grad: float32 [48], P('tensor')
- decay_log_grad: float32 [48], P('tensor')
- skip_weight_grad: float32 [48], P('tensor')
- gated_norm_weight_grad: float32 [3072], P('tensor')
- out_proj_grad: float32 [3072, 1536], P('tensor')
The draws below stay inside these ranges and needn't reach their ends.
Inputs may be any that keep to these rules, and one draw needn't show every extreme that they name: `segments`: within a sequence document numbers never fall, each document is a run of 1 to 256 tokens, and one has exactly 256.
All inputs are finite; a program needn't handle non-finite values.
Results may differ from the reference program's by a relative error of at most 0.0081.
Values may be sent and summed in bfloat16 or wider, within the bound.
No kernel may reach another device: no remote copies, remote signals or barrier semaphores. Data moves between devices by JAX's collectives and lax.ppermute only.
A program may use at most 128 MiB of HBM per device.

```python
import math
import jax
import jax.numpy as jnp
import numpy as np
from jax import lax

D = 1536
HEADS = 48
HEADDIM = 64
NSTATE = 128
KERNEL = 4
GROUP = 256
SEQ_LEN = 512
INNER = 3072
SEQS = 16
DOCS = 3
DOC_MOST = 256


def level_of(stream_key, shape, cuts, smallest, largest):
    factor_of = 1.0
    for position, parts in cuts:
        heights = jax.random.uniform(jax.random.fold_in(jax.random.fold_in(stream_key, 6), position), (parts,), jnp.float32, smallest / len(cuts), largest / len(cuts))
        factor_of = factor_of * jnp.repeat(jnp.exp(heights), shape[position] // parts).reshape((-1,) + (1,) * (len(shape) - 1 - position))
    return factor_of


def split_up(count, total, most, skew):
    weights = [(1 << 20) // math.isqrt(standing ** skew) + 1 for standing in range(2, count + 1)]
    spare, counts = total - most - (count - 1), [1] * (count - 1)
    while spare > 0:
        free = [i for i in range(count - 1) if counts[i] < most]
        mass, left = sum([weights[i] for i in free]), spare
        for i in free:
            addition = min(most - counts[i], max(1, left * weights[i] // mass), spare)
            counts[i] = counts[i] + addition
            spare = spare - addition
    return np.array([most] + counts)


def ragged(key, number_of, total, reach, lean):
    if number_of == 2:
        one = jax.random.randint(key, (), max(1, total - reach), min(reach, total - 1) + 1)
        return jnp.stack([one, total - one])
    sizes = jnp.asarray(split_up(number_of, total, reach, lean), jnp.int32)
    couples = (number_of - 1) // 2
    giver, sink = sizes[1:1 + 2 * couples:2], sizes[2:2 + 2 * couples:2]
    slack = jnp.minimum(giver - 1, reach - sink)
    moved = jax.random.randint(jax.random.fold_in(key, 1), (couples,), 0, 1 << 20) % (slack + 1)
    sizes = sizes.at[1:1 + 2 * couples:2].set(giver - moved).at[2:2 + 2 * couples:2].set(sink + moved)
    return sizes[jax.random.permutation(jax.random.fold_in(key, 2), number_of)]


def gaussian(key, extent, scale, limit, split=(), held_as=jnp.bfloat16):
    drawn = jax.random.normal(key, extent, jnp.float32) * scale
    if len(split) > 0:
        drawn = level_of(key, extent, split, -0.22, 0.18) * drawn
    return jnp.clip(drawn, min=-limit, max=limit).astype(held_as)


def setup_inputs(seed: int = 0) -> dict:
    splits = jax.random.split(jax.random.key(seed), 18)
    inputs = gaussian(splits[0], (SEQS, SEQ_LEN, D), 1.0, 6.0, ((0, 16),))
    norm_weight = jnp.clip(1.0 + 0.1 * jax.random.normal(splits[1], (D,), jnp.float32), 0.5, 1.5)
    gate_proj = gaussian(splits[2], (D, INNER), D ** -0.5, 0.15625, ((1, 8),))
    inner_proj = gaussian(splits[3], (D, INNER), D ** -0.5, 0.15625, ((1, 8),))
    state_proj = gaussian(splits[4], (D, 2 * NSTATE), D ** -0.5, 0.15625)
    step_proj = gaussian(splits[5], (D, HEADS), D ** -0.5, 0.15625, ((1, 8),))
    inner_conv = gaussian(splits[6], (KERNEL, INNER), KERNEL ** -0.5, 3.0, ((1, 8),), jnp.float32)
    inner_conv_bias = gaussian(splits[7], (INNER,), 0.3, 1.5, ((0, 8),), jnp.float32)
    state_conv = gaussian(splits[8], (KERNEL, 2 * NSTATE), KERNEL ** -0.5, 3.0, (), jnp.float32)
    state_conv_bias = gaussian(splits[9], (2 * NSTATE,), 0.3, 1.5, (), jnp.float32)
    step_bias = jnp.clip(-6.9 + 4.65 * jax.random.uniform(splits[10], (HEADS,), jnp.float32) ** level_of(splits[10], (HEADS,), ((0, 8),), -0.2, 0.2), -6.9, -2.25)
    decay_log = jnp.clip(2.77 * jax.random.uniform(splits[11], (HEADS,), jnp.float32) ** level_of(splits[11], (HEADS,), ((0, 8),), -0.2, 0.2), 0.0, 2.77)
    skip_weight = jnp.clip(0.5 + 1.0 * jax.random.uniform(splits[12], (HEADS,), jnp.float32) ** level_of(splits[12], (HEADS,), ((0, 8),), -0.2, 0.2), 0.5, 1.5)
    gated_norm_weight = jnp.clip(1.0 + 0.1 * jax.random.normal(splits[13], (INNER,), jnp.float32), 0.5, 1.5)
    out_proj = gaussian(splits[14], (INNER, D), INNER ** -0.5, 0.109375, ((0, 8),))
    segments = jax.vmap(lambda own: jnp.searchsorted(jnp.cumsum(ragged(own, DOCS, SEQ_LEN, DOC_MOST, 0)), jnp.arange(SEQ_LEN), side="right"))(jax.random.split(splits[15], SEQS)).reshape((SEQS, SEQ_LEN)).astype(jnp.int32)
    cotangent = gaussian(splits[16], (SEQS, SEQ_LEN, D), 1.0, 6.0, ((0, 16),))
    return dict(inputs=inputs, norm_weight=norm_weight, gate_proj=gate_proj, inner_proj=inner_proj, state_proj=state_proj, step_proj=step_proj, inner_conv=inner_conv, inner_conv_bias=inner_conv_bias, state_conv=state_conv, state_conv_bias=state_conv_bias, step_bias=step_bias, decay_log=decay_log, skip_weight=skip_weight, gated_norm_weight=gated_norm_weight, out_proj=out_proj, segments=segments, cotangent=cotangent)


@jax.custom_vjp
def low(v):
    return lax.optimization_barrier(v.astype(jnp.bfloat16)).astype(jnp.float32)

@jax.custom_vjp
def low_back(v):
    return v

def low_keep(v):
    return (low(v), None)

def low_pass(kept, grad):
    return (grad,)

def back_keep(v):
    return (v, None)

def back_low(kept, grad):
    return (low(grad),)
low.defvjp(low_keep, low_pass)
low_back.defvjp(back_keep, back_low)
epsilon = 1e-05
precise = lax.Precision.HIGHEST

def product(left, right):
    return jnp.dot(left, right, precision=precise, preferred_element_type=jnp.float32)

def masked_conv(values, weights, bias, segs):
    length = values.shape[0]
    total = bias[None, :] + weights[0][None, :] * values
    for offset in range(1, KERNEL):
        earlier = jnp.concatenate([jnp.zeros((offset, values.shape[1]), jnp.float32), values[:length - offset]], axis=0)
        earlier_seg = jnp.concatenate([jnp.full((offset,), -1, jnp.int32), segs[:length - offset]], axis=0)
        same = (earlier_seg == segs).astype(jnp.float32)
        total = total + weights[offset][None, :] * earlier * same[:, None]
    return jax.nn.silu(total)

def group_body(carry, pieces, rate):
    state, previous = carry
    head_in, b_block, c_block, step_block, seg_block = pieces
    block = seg_block.shape[0]
    logs = jnp.cumsum(step_block * rate[None, :], axis=0)
    row_ids = lax.broadcasted_iota(jnp.int32, (block, block), 0)
    col_ids = lax.broadcasted_iota(jnp.int32, (block, block), 1)
    linked = (seg_block[:, None] == seg_block[None, :]) & (row_ids >= col_ids)
    spread = jnp.where(linked[:, :, None], logs[:, None, :] - logs[None, :, :], 0.0)
    decay = jnp.exp(spread) * linked[:, :, None].astype(jnp.float32)
    scores = jnp.dot(c_block, b_block.T, precision=precise, preferred_element_type=jnp.float32)
    inflow = head_in * step_block[:, :, None]
    within = jnp.einsum('ijh,jhp->ihp', scores[:, :, None] * decay, inflow, precision=precise)
    carried = (seg_block == previous).astype(jnp.float32)
    entering = jnp.einsum('in,hpn->ihp', c_block, state, precision=precise) * (jnp.exp(logs) * carried[:, None])[:, :, None]
    final_seg = seg_block[block - 1]
    keeping = (seg_block == final_seg).astype(jnp.float32)
    tail = jnp.exp(logs[block - 1][None, :] - logs) * keeping[:, None]
    survive = jnp.exp(logs[block - 1]) * (final_seg == previous).astype(jnp.float32)
    new_state = state * survive[:, None, None] + jnp.einsum('jh,jhp,jn->hpn', tail, inflow, b_block, precision=precise)
    return ((new_state, final_seg), within + entering)

def state_space(heads_in, bmat, cmat, step, rate, segs):
    length, heads, headdim = heads_in.shape
    blocks = length // GROUP
    pieces = (heads_in.reshape(blocks, GROUP, heads, headdim), bmat.reshape(blocks, GROUP, -1), cmat.reshape(blocks, GROUP, -1), step.reshape(blocks, GROUP, heads), segs.reshape(blocks, GROUP))

    def advance(carry, piece):
        return group_body(carry, piece, rate)
    start = (jnp.zeros((heads, headdim, bmat.shape[1]), jnp.float32), jnp.array(-1, jnp.int32))
    _, mixed = lax.scan(jax.checkpoint(advance), start, pieces)
    return mixed.reshape(length, heads, headdim)

def forward(values, params, segs):
    norm_weight, gate_proj, inner_proj, state_proj, step_proj, inner_conv, inner_conv_bias, state_conv, state_conv_bias, step_bias, decay_log, skip_weight, gated_norm_weight, out_proj = params
    length = values.shape[0]
    in_scale = lax.rsqrt(lax.optimization_barrier(jnp.mean(values * values, axis=1, keepdims=True)) + epsilon)
    normed = low(values * in_scale * norm_weight[None, :])
    gate = low_back(product(normed, gate_proj))
    inner = low_back(product(normed, inner_proj))
    states_in = low_back(product(normed, state_proj))
    step_raw = low_back(product(normed, step_proj))
    conv_inner = masked_conv(inner, inner_conv, inner_conv_bias, segs)
    conv_states = masked_conv(states_in, state_conv, state_conv_bias, segs)
    step = jax.nn.softplus(step_raw + step_bias[None, :])
    heads_in = conv_inner.reshape(length, HEADS, HEADDIM)
    mixed = state_space(heads_in, conv_states[:, :NSTATE], conv_states[:, NSTATE:], step, -jnp.exp(decay_log), segs)
    mixed = mixed + skip_weight[None, :, None] * heads_in
    gated = mixed.reshape(length, INNER) * jax.nn.silu(gate)
    out_scale = lax.rsqrt(lax.optimization_barrier(jnp.mean(gated * gated, axis=1, keepdims=True)) + epsilon)
    normed_out = low(gated * out_scale * gated_norm_weight[None, :])
    return values + product(normed_out, out_proj)

def reference(inputs, norm_weight, gate_proj, inner_proj, state_proj, step_proj, inner_conv, inner_conv_bias, state_conv, state_conv_bias, step_bias, decay_log, skip_weight, gated_norm_weight, out_proj, segments, cotangent):
    weights = (norm_weight, gate_proj.astype(jnp.float32), inner_proj.astype(jnp.float32), state_proj.astype(jnp.float32), step_proj.astype(jnp.float32), inner_conv, inner_conv_bias, state_conv, state_conv_bias, step_bias, decay_log, skip_weight, gated_norm_weight, out_proj.astype(jnp.float32))

    def one_sequence(totals, pieces):
        values, segs, grad_out = pieces

        def apply(values, params):
            return forward(values, params, segs)
        result, pull = jax.vjp(apply, values, weights)
        value_grad, param_grads = pull(grad_out)
        totals = jax.tree.map(jnp.add, totals, param_grads)
        return (totals, (result.astype(jnp.bfloat16), value_grad))
    zeros = jax.tree.map(jnp.zeros_like, weights)
    totals, (outputs, input_grad) = lax.scan(one_sequence, zeros, (inputs.astype(jnp.float32), segments, cotangent.astype(jnp.float32)))
    return (outputs, input_grad, totals[0], totals[1], totals[2], totals[3], totals[4], totals[5], totals[6], totals[7], totals[8], totals[9], totals[10], totals[11], totals[12], totals[13])
```

```python
import functools

import jax
import jax.numpy as jnp
from jax import lax
from jax.experimental import pallas as pl
from jax.experimental.pallas import tpu as pltpu
from jax.sharding import Mesh, PartitionSpec as P

KERNEL = 4
INNER = 3072
EPS = 1e-05
T = 512
GROUP = 256
D = 1536
C = 384
NH = 6
HD = 64
N = 128
BF = jnp.bfloat16
F32 = jnp.float32
EXACT = lax.Precision.HIGHEST
VM = pl.BlockSpec(memory_space=pltpu.VMEM)


def dot(a, b, precision=None):
    return jnp.dot(a, b, preferred_element_type=F32, precision=precision)


def dot_nt(a, b):
    return lax.dot_general(a, b, (((1,), (1,)), ((), ())), preferred_element_type=F32)


def dot_tn(a, b):
    return lax.dot_general(a, b, (((0,), (0,)), ((), ())), preferred_element_type=F32)


def sigmoid(v):
    return 1.0 / (1.0 + jnp.exp(-v))


def softplus(v):
    return jnp.maximum(v, 0.0) + jnp.log1p(jnp.exp(-jnp.abs(v)))


def lane_ids(rows, cols):
    return lax.broadcasted_iota(jnp.int32, (rows, cols), 1)


def row_ids(rows, cols):
    return lax.broadcasted_iota(jnp.int32, (rows, cols), 0)


def conv_masks(seg):
    lanes = lane_ids(1, T)
    out = []
    for k in range(1, KERNEL):
        same = (pltpu.roll(seg, k, 1) == seg) & (lanes >= k)
        out.append(same.astype(F32))
    return out


def conv_forward(v, cols, bias, masks):
    total = bias + cols[0] * v
    for k in range(1, KERNEL):
        total = total + cols[k] * (pltpu.roll(v, k, 1) * masks[k - 1])
    return total


def conv_backward(d_pre, v, cols, masks):
    d_v = cols[0] * d_pre
    taps = [jnp.sum(d_pre * v, axis=1, keepdims=True)]
    for k in range(1, KERNEL):
        back = pltpu.roll(d_pre * masks[k - 1], T - k, 1)
        d_v = d_v + cols[k] * back
        taps.append(jnp.sum(back * v, axis=1, keepdims=True))
    return d_v, taps, jnp.sum(d_pre, axis=1, keepdims=True)


def scan_logs(step, rate, rows_ref, seg):
    upper = (row_ids(GROUP, GROUP) <= lane_ids(GROUP, GROUP)).astype(F32)
    a = step * rate
    logs = jnp.concatenate(
        [dot(a[:, :GROUP], upper, EXACT), dot(a[:, GROUP:], upper, EXACT)], axis=1
    )
    rows_ref[...] = jnp.zeros_like(rows_ref)
    rows_ref[0:8, :] = logs
    rows_ref[8:9, :] = seg.astype(F32)
    return logs, rows_ref[...].T


def link_mask(cols, segf, c):
    sl = slice(c * GROUP, (c + 1) * GROUP)
    same = cols[sl, 8:9] == segf[:, sl]
    later = lane_ids(GROUP, GROUP) >= row_ids(GROUP, GROUP)
    return jnp.where(same & later, 0.0, -1e30)


def state_rows(logs, segf):
    final = segf[:, GROUP - 1 : GROUP]
    tail = jnp.exp(logs[:, GROUP - 1 : GROUP] - logs[:, :GROUP]) * (
        segf[:, :GROUP] == final
    ).astype(F32)
    entry = jnp.exp(logs[:, GROUP:]) * (segf[:, GROUP:] == final).astype(F32)
    return tail, entry


def per_head(rows, width):
    return jnp.concatenate(
        [jnp.broadcast_to(rows[h : h + 1, :], (HD, width)) for h in range(NH)], axis=0
    )


def fwd_kernel(
    x_ref, cot_ref, nw_ref, gp_ref, ip_ref, sp_ref, tp_ref, ic_ref, icb_ref, sc_ref, scb_ref,
    tb_ref, dl_ref, sk_ref, gnw_ref, op_ref, seg_ref,
    normed_ref, gate_ref, inner_ref, pre_ref, mixed_ref, dno_ref, states_ref, spre_ref,
    raw_ref, cols_ref, scols_ref, head_ref, sums_ref,
    tpad, rows_scr, par_scr, u_scr,
):
    def norm_block(r, _):
        sl = pl.ds(r * 32, 32)
        v = x_ref[sl, :].astype(F32)
        scale = lax.rsqrt(jnp.mean(v * v, axis=1, keepdims=True) + EPS)
        normed_ref[sl, :] = (v * scale * nw_ref[...]).astype(BF)
        return 0

    lax.fori_loop(0, T // 32, norm_block, 0)
    par_scr[...] = jnp.zeros_like(par_scr)
    par_scr[0:4, 0:C] = ic_ref[...]
    par_scr[4:5, 0:C] = icb_ref[...]
    par_scr[5:6, 0:C] = gnw_ref[...]
    par_scr[0:4, C : C + 256] = sc_ref[...]
    par_scr[4:5, C : C + 256] = scb_ref[...]
    par_scr[8:9, 0:NH] = tb_ref[...]
    par_scr[9:10, 0:NH] = dl_ref[...]
    par_scr[10:11, 0:NH] = sk_ref[...]
    par = par_scr[...].T
    cols_ref[...] = par[0:C, 0:8]
    scols_ref[...] = par[C : C + 256, 0:8]
    head_ref[...] = par[0:8, :]
    tpad[...] = jnp.zeros_like(tpad)
    tpad[:, 0:NH] = tp_ref[...]
    normed = normed_ref[...]
    gate_ref[...] = dot(normed, gp_ref[...]).T
    inner_ref[...] = dot(normed, ip_ref[...]).T
    states_ref[...] = dot(normed, sp_ref[...]).T
    raw_ref[...] = dot(normed, tpad[...]).T[0:8, :]
    dno_ref[...] = dot_nt(op_ref[...], cot_ref[...])

    seg = seg_ref[...]
    segf = seg.astype(F32)
    masks = conv_masks(seg)
    head = head_ref[...]
    step = softplus(raw_ref[...] + head[:, 8:9])
    rate = -jnp.exp(head[:, 9:10])
    logs, lcols = scan_logs(step, rate, rows_scr, seg)

    sv = states_ref[...]
    spre = conv_forward(
        sv, [scols_ref[:, k : k + 1] for k in range(KERNEL)], scols_ref[:, 4:5], masks
    )
    spre_ref[...] = spre
    cs = spre * sigmoid(spre)
    b_tok = cs[0:N, :].T.astype(BF)
    c_low = cs[N:, :].astype(BF)
    for h in range(NH):
        hs = slice(h * HD, (h + 1) * HD)
        pre = conv_forward(
            inner_ref[hs, :], [cols_ref[hs, k : k + 1] for k in range(KERNEL)],
            cols_ref[hs, 4:5], masks,
        )
        pre_ref[hs, :] = pre
        u_scr[hs, :] = pre * sigmoid(pre)
    tail, entry = state_rows(logs, segf)
    weighted = u_scr[:, 0:GROUP] * per_head(step[:, 0:GROUP] * tail, GROUP)
    state = dot(weighted.astype(BF), b_tok[0:GROUP, :])
    entering = dot(state.astype(BF), c_low[:, GROUP:])
    for c in range(2):
        sl = slice(c * GROUP, (c + 1) * GROUP)
        neg = link_mask(lcols, segf, c)
        scores = dot(b_tok[sl, :], c_low[:, sl])
        for h in range(NH):
            hs = slice(h * HD, (h + 1) * HD)
            decay = jnp.exp((logs[h : h + 1, sl] - lcols[sl, h : h + 1]) + neg)
            m = (scores * decay).astype(BF)
            u = u_scr[hs, sl]
            y = dot((u * step[h : h + 1, sl]).astype(BF), m)
            if c == 1:
                y = y + entering[hs, :] * entry[h : h + 1, :]
            mixed_ref[hs, sl] = y + head[h : h + 1, 10:11] * u
    squares = jnp.zeros((1, T), F32)
    dots = jnp.zeros((1, T), F32)
    for h in range(NH):
        hs = slice(h * HD, (h + 1) * HD)
        g = gate_ref[hs, :]
        gated = mixed_ref[hs, :] * (g * sigmoid(g))
        squares = squares + jnp.sum(gated * gated, axis=0, keepdims=True)
        dots = dots + jnp.sum(dno_ref[hs, :] * cols_ref[hs, 5:6] * gated, axis=0, keepdims=True)
    sums_ref[0:1, :] = squares
    sums_ref[1:2, :] = dots


def sds(shape, dtype):
    return jax.ShapeDtypeStruct(shape, dtype)


def call(kernel, outs, args, scratch=(), smem=0, cost=(0, 0), name=None):
    specs = [pl.BlockSpec(memory_space=pltpu.SMEM)] * smem + [VM] * (len(args) - smem)
    return pl.pallas_call(
        kernel,
        out_shape=outs,
        in_specs=specs,
        out_specs=jax.tree.map(lambda _: VM, outs),
        scratch_shapes=list(scratch),
        compiler_params=pltpu.CompilerParams(vmem_limit_bytes=48 << 20),
        cost_estimate=pl.CostEstimate(flops=cost[0], bytes_accessed=cost[1], transcendentals=0),
        name=name,
    )(*args)


def forward(*args):
    outs = [
        sds((T, D), BF), sds((C, T), F32), sds((C, T), F32), sds((C, T), F32), sds((C, T), F32),
        sds((C, T), F32), sds((256, T), F32), sds((256, T), F32), sds((8, T), F32),
        sds((C, 8), F32), sds((256, 8), F32), sds((8, 128), F32), sds((2, T), F32),
    ]
    scratch = [
        pltpu.VMEM((D, 128), BF), pltpu.VMEM((128, T), F32), pltpu.VMEM((128, 640), F32),
        pltpu.VMEM((C, T), F32),
    ]
    return call(fwd_kernel, outs, args, scratch, 0, (6_000_000_000, 16_000_000), "forward")


def mid_kernel(
    sums_ref, gate_ref, mixed_ref, dno_ref, cols_ref, cot_ref, normed_ref,
    out_grad_ref, gate_grad_ref, no_ref, gate_low_ref, dy_ref, gain_ref,
    no_scr, low_scr,
):
    total = jnp.sum(sums_ref[...], axis=0)
    scale = lax.rsqrt(total[0:1, :] / INNER + EPS)
    slope = scale * scale * scale * (total[1:2, :] / INNER)
    for h in range(NH):
        hs = slice(h * HD, (h + 1) * HD)
        g = gate_ref[hs, :]
        s = sigmoid(g)
        silu = g * s
        mixed = mixed_ref[hs, :]
        gated = mixed * silu
        gain = cols_ref[hs, 5:6]
        normal = gated * scale
        no_scr[hs, :] = (normal * gain).astype(BF)
        dno = dno_ref[hs, :]
        gain_ref[hs, :] = jnp.broadcast_to(jnp.sum(dno * normal, axis=1, keepdims=True), (HD, 8))
        d_gated = scale * (dno * gain) - gated * slope
        low_scr[hs, :] = (d_gated * mixed * (s * (1.0 + g * (1.0 - s)))).astype(BF)
        dy_ref[hs, :] = d_gated * silu
    out_grad_ref[...] = dot(no_scr[...], cot_ref[...]).astype(out_grad_ref.dtype)
    gate_grad_ref[...] = dot(low_scr[...], normed_ref[...]).astype(gate_grad_ref.dtype)
    no_ref[...] = no_scr[...].T
    gate_low_ref[...] = low_scr[...].T


def middle(*args):
    outs = [
        sds((C, D), F32), sds((C, D), BF), sds((T, C), BF), sds((T, C), BF), sds((C, T), F32),
        sds((C, 8), F32),
    ]
    scratch = [pltpu.VMEM((C, T), BF), pltpu.VMEM((C, T), BF)]
    return call(mid_kernel, outs, args, scratch, 0, (3_000_000_000, 12_000_000), "middle")


def bwd_kernel(
    idx_ref, inner_ref, pre_ref, dy_ref, spre_ref, raw_ref, cols_ref, head_ref, seg_ref, normed_ref,
    inner_grad_ref, step_grad_ref, inner_low_ref, step_low_ref, give_ref, keep_ref, small_ref,
    heads_ref,
    rows_scr, u_scr, di_scr, low_scr,
):
    seg = seg_ref[...]
    segf = seg.astype(F32)
    masks = conv_masks(seg)
    head = head_ref[...]
    raw = raw_ref[...] + head[:, 8:9]
    step = softplus(raw)
    rate = -jnp.exp(head[:, 9:10])
    logs, lcols = scan_logs(step, rate, rows_scr, seg)
    spre = spre_ref[...]
    cs = spre * sigmoid(spre)
    b_low = cs[0:N, :].astype(BF)
    c_low = cs[N:, :].astype(BF)
    b_tok = cs[0:N, :].T.astype(BF)
    c_tok = cs[N:, :].T.astype(BF)
    for h in range(NH):
        hs = slice(h * HD, (h + 1) * HD)
        pre = pre_ref[hs, :]
        u_scr[hs, :] = pre * sigmoid(pre)
    tail, entry = state_rows(logs, segf)
    first, second = slice(0, GROUP), slice(GROUP, T)
    weighted = (u_scr[:, first] * per_head(step[:, first] * tail, GROUP)).astype(BF)
    state = dot(weighted, b_tok[first, :]).astype(BF)
    d_entering = (dy_ref[:, second] * per_head(entry, GROUP)).astype(BF)
    d_state = dot(d_entering, c_tok[second, :]).astype(BF)
    entering = dot(state, c_low[:, second])
    into = dot(d_state, b_low[:, first])
    d_c_second = dot_tn(state, d_entering)
    d_b_first = dot_tn(d_state, weighted)
    tri = (row_ids(GROUP, GROUP) >= lane_ids(GROUP, GROUP)).astype(BF)
    before = (row_ids(GROUP, GROUP) < lane_ids(GROUP, GROUP)).astype(F32)
    upto = (row_ids(GROUP, GROUP) < lane_ids(GROUP, GROUP)).astype(F32)
    since = (row_ids(GROUP, GROUP) >= lane_ids(GROUP, GROUP)).astype(F32)
    out_step = []
    out_skip = []
    da_rows = [[None, None] for _ in range(NH)]
    for c in range(2):
        sl = slice(c * GROUP, (c + 1) * GROUP)
        neg = link_mask(lcols, segf, c)
        scores = dot(b_tok[sl, :], c_low[:, sl])
        d_scores = jnp.zeros((GROUP, GROUP), F32)
        for h in range(NH):
            hs = slice(h * HD, (h + 1) * HD)
            decay = jnp.exp((logs[h : h + 1, sl] - lcols[sl, h : h + 1]) + neg)
            m = scores * decay
            dy = dy_ref[hs, sl].astype(BF)
            inflow = (u_scr[hs, sl] * step[h : h + 1, sl]).astype(BF)
            g = dot_tn(inflow, dy)
            d_scores = d_scores + g * decay
            w = dot((g * m).astype(BF), tri)
            da = jnp.sum(w * before, axis=0, keepdims=True)
            da_rows[h][c] = da
            di = dot_nt(dy, m.astype(BF))
            if c == 0:
                di = di + into[hs, :] * tail[h : h + 1, :]
            di_scr[hs, sl] = di
        ds = d_scores.astype(BF)
        d_b = dot_nt(c_low[:, sl], ds)
        d_c = dot(b_low[:, sl], ds)
        if c == 0:
            d_b = d_b + d_b_first
        else:
            d_c = d_c + d_c_second
        give_ref[:, sl] = jnp.where(idx_ref[0] == 0, d_c, d_b).astype(BF)
        keep_ref[:, sl] = jnp.where(idx_ref[0] == 0, d_b, d_c).astype(BF)
    zero = jnp.zeros((1, GROUP), F32)
    q_rows, e_rows = [], []
    for h in range(NH):
        hs = slice(h * HD, (h + 1) * HD)
        q = u_scr[hs, first] * step[h : h + 1, first] * into[hs, :]
        q_rows.append(jnp.sum(q, axis=0, keepdims=True))
        e = dy_ref[hs, second] * entering[hs, :]
        e_rows.append(jnp.sum(e, axis=0, keepdims=True))
    q8 = jnp.concatenate(q_rows + [zero, zero], axis=0) * tail
    e8 = jnp.concatenate(e_rows + [zero, zero], axis=0) * entry
    da0 = jnp.concatenate([da_rows[h][0] for h in range(NH)] + [zero, zero], axis=0)
    da1 = jnp.concatenate([da_rows[h][1] for h in range(NH)] + [zero, zero], axis=0)
    da = jnp.concatenate([da0 + dot(q8, upto, EXACT), da1 + dot(e8, since, EXACT)], axis=1)
    d_steps = []
    for h in range(NH):
        hs = slice(h * HD, (h + 1) * HD)
        pre = pre_ref[hs, :]
        s = sigmoid(pre)
        u = u_scr[hs, :]
        di = di_scr[hs, :]
        dy = dy_ref[hs, :]
        d_steps.append(jnp.sum(di * u, axis=0, keepdims=True))
        out_skip.append(jnp.sum(dy * u, axis=0, keepdims=True))
        d_u = di * step[h : h + 1, :] + head[h : h + 1, 10:11] * dy
        d_pre = d_u * (s * (1.0 + pre * (1.0 - s)))
        d_v, taps, bias = conv_backward(
            d_pre, inner_ref[hs, :], [cols_ref[hs, k : k + 1] for k in range(KERNEL)], masks
        )
        low_scr[hs, :] = d_v.astype(BF)
        for k in range(KERNEL):
            small_ref[hs, k : k + 1] = taps[k]
        small_ref[hs, 4:5] = bias
    zero = jnp.zeros((2, T), F32)
    d_step = jnp.concatenate(d_steps + [zero], axis=0) + da * rate
    skips = jnp.concatenate(out_skip + [zero], axis=0)
    d_raw = d_step * sigmoid(raw)
    heads_ref[...] = jnp.zeros_like(heads_ref)
    heads_ref[:, 0:1] = jnp.sum(d_raw, axis=1, keepdims=True)
    heads_ref[:, 1:2] = jnp.sum(da * step, axis=1, keepdims=True) * rate
    heads_ref[:, 2:3] = jnp.sum(skips, axis=1, keepdims=True)
    rows_scr[...] = jnp.zeros_like(rows_scr)
    rows_scr[0:8, :] = d_raw
    step_low_ref[...] = rows_scr[...].T.astype(BF)
    step_grad_ref[...] = dot(d_raw.astype(BF), normed_ref[...])
    inner_grad_ref[...] = dot(low_scr[...], normed_ref[...]).astype(inner_grad_ref.dtype)
    inner_low_ref[...] = low_scr[...].T


def backward(*args):
    outs = [
        sds((C, D), BF), sds((8, D), F32), sds((T, C), BF), sds((T, 128), BF), sds((128, T), BF),
        sds((128, T), BF), sds((C, 8), F32), sds((8, 128), F32),
    ]
    scratch = [
        pltpu.VMEM((128, T), F32), pltpu.VMEM((C, T), F32), pltpu.VMEM((C, T), F32),
        pltpu.VMEM((C, T), BF),
    ]
    return call(bwd_kernel, outs, args, scratch, 1, (6_000_000_000, 10_000_000), "backward")


def tail_kernel(
    idx_ref, p0_ref, p1_ref, p2_ref, p3_ref, states_ref, spre_ref, scols_ref, seg_ref, normed_ref,
    gate_low_ref, inner_low_ref, step_low_ref, gp_ref, ip_ref, tp_ref, sp_ref, step_grad_ref,
    small_ref, heads_ref, gain_ref,
    give_ref, keep_ref, pack_ref,
    tpad, low_scr, tok_scr, pad_scr,
):
    core = idx_ref[0]
    own = pl.ds(pl.multiple_of(core * 128 + idx_ref[1] * 32, 32), 32)
    masks = conv_masks(seg_ref[...])
    d_cs = (p0_ref[...] + p1_ref[...].astype(F32)) + (
        p2_ref[...].astype(F32) + p3_ref[...].astype(F32)
    )
    pre = spre_ref[own, :]
    s = sigmoid(pre)
    d_pre = d_cs * (s * (1.0 + pre * (1.0 - s)))
    cols = scols_ref[own, :]
    d_v, taps, bias = conv_backward(
        d_pre, states_ref[own, :], [cols[:, k : k + 1] for k in range(KERNEL)], masks
    )
    low_scr[...] = jnp.zeros_like(low_scr)
    low_scr[own, :] = d_v
    tok_scr[...] = low_scr[...].T.astype(BF)
    pack_ref[0:32, :] = dot(d_v.astype(BF), normed_ref[...]).astype(pack_ref.dtype)
    pad_scr[...] = jnp.zeros_like(pad_scr)
    pad_scr[0:C, 0:8] = small_ref[...]
    pad_scr[0:C, 5:6] = gain_ref[:, 0:1]
    for k in range(KERNEL):
        pad_scr[C : C + 32, k : k + 1] = taps[k]
    pad_scr[C : C + 32, 4:5] = bias
    rows = pad_scr[...].T[0:8, :]
    pack_ref[32:40, :] = step_grad_ref[...].astype(pack_ref.dtype)
    pack_ref[40:48, 0:512] = rows.astype(pack_ref.dtype)
    pack_ref[40:48, 512:640] = heads_ref[...].astype(pack_ref.dtype)
    pack_ref[40:48, 640:] = jnp.zeros((8, D - 640), pack_ref.dtype)
    tpad[...] = jnp.zeros_like(tpad)
    tpad[:, 0:NH] = tp_ref[...]
    for ref, half in ((give_ref, 1 - core), (keep_ref, core)):
        tok = pl.ds(pl.multiple_of(half * GROUP, GROUP), GROUP)
        total = dot_nt(gate_low_ref[tok, :], gp_ref[...])
        total = total + dot_nt(inner_low_ref[tok, :], ip_ref[...])
        total = total + dot_nt(tok_scr[tok, :], sp_ref[...])
        total = total + dot_nt(step_low_ref[tok, :], tpad[...])
        ref[...] = total.astype(BF)


def tail(*args):
    outs = [sds((GROUP, D), BF), sds((GROUP, D), BF), sds((48, D), BF)]
    scratch = [
        pltpu.VMEM((D, 128), BF), pltpu.VMEM((256, T), F32), pltpu.VMEM((T, 256), BF),
        pltpu.VMEM((512, 128), F32),
    ]
    return call(tail_kernel, outs, args, scratch, 1, (3_500_000_000, 10_000_000), "tail")


def product_kernel(idx_ref, no_ref, op_ref, give_ref, keep_ref):
    core = idx_ref[0]
    for ref, half in ((give_ref, 1 - core), (keep_ref, core)):
        tok = pl.ds(pl.multiple_of(half * GROUP, GROUP), GROUP)
        ref[...] = dot(no_ref[tok, :], op_ref[...]).astype(BF)


def product(*args):
    outs = [sds((GROUP, D), BF), sds((GROUP, D), BF)]
    return call(product_kernel, outs, args, (), 1, (1_500_000_000, 4_000_000), "product")


def fold_kernel(idx_ref, keep_ref, got_ref, own_ref, *send_refs):
    rows = own_ref.shape[0]
    for k in range(4):
        sl = pl.ds(pl.multiple_of(lax.rem(idx_ref[1] + k, 4) * rows, rows), rows)
        v = keep_ref[sl, :].astype(F32) + got_ref[sl, :].astype(F32)
        if k == 0:
            own_ref[...] = v
        else:
            send_refs[k - 1][...] = v.astype(BF)


def scatter(idx, give, keep):
    got = lax.ppermute(give, "core", [(0, 1), (1, 0)])
    rows, width = keep.shape[0] // 4, keep.shape[1]
    outs = [sds((rows, width), F32)] + [sds((rows, width), BF)] * 3
    own, *sends = call(fold_kernel, outs, (idx, keep, got), (), 1, (2_000_000, 2_000_000), "fold")
    return [own] + [turn(send, "y", k + 1) for k, send in enumerate(sends)]


def turn(v, axis, by):
    return lax.ppermute(v, axis, [(i, (i + by) % 4) for i in range(4)])


def join_kernel(idx_ref, *refs):
    out_ref = refs[4]
    rows = refs[0].shape[0]
    for k in range(4):
        slot = lax.rem(idx_ref[1] + 4 - k, 4)
        out_ref[pl.ds(pl.multiple_of(slot * rows, rows), rows), :] = refs[k][...]


def finish_kernel(idx_ref, mine_ref, other_ref, out_ref):
    rows = mine_ref.shape[0]
    core = idx_ref[0]
    out_ref[pl.ds(pl.multiple_of(core * rows, rows), rows), :] = mine_ref[...].astype(out_ref.dtype)
    out_ref[pl.ds(pl.multiple_of((1 - core) * rows, rows), rows), :] = other_ref[...].astype(
        out_ref.dtype
    )


def gather(idx, chunk, dtype):
    rows, width = chunk.shape
    pieces = [chunk] + [turn(chunk, "y", k) for k in range(1, 4)]
    half = call(join_kernel, sds((4 * rows, width), BF), (idx, *pieces), (), 1, (0, 2_000_000), "join")
    other = lax.ppermute(half, "core", [(0, 1), (1, 0)])
    return call(
        finish_kernel, sds((8 * rows, width), dtype), (idx, half, other), (), 1, (0, 4_000_000), "finish"
    )


def input_kernel(p0, p1, p2, p3, x_ref, cot_ref, nw_ref, ig_ref, norm_ref):
    d_normed = (p0[...] + p1[...].astype(F32)) + (p2[...].astype(F32) + p3[...].astype(F32))
    v = x_ref[...].astype(F32)
    scale = lax.rsqrt(jnp.mean(v * v, axis=1, keepdims=True) + EPS)
    weighted = d_normed * nw_ref[...]
    grad = scale * weighted - v * (
        scale * scale * scale * jnp.mean(weighted * v, axis=1, keepdims=True)
    )
    ig_ref[...] = (cot_ref[...].astype(F32) + grad).astype(BF)
    norm_ref[...] = jnp.broadcast_to(
        jnp.sum(d_normed * v * scale, axis=0, keepdims=True), norm_ref.shape
    ).astype(BF)


def output_kernel(p0, p1, p2, p3, x_ref, out_ref):
    total = (p0[...] + p1[...].astype(F32)) + (p2[...].astype(F32) + p3[...].astype(F32))
    out_ref[...] = (x_ref[...].astype(F32) + total).astype(BF)


def order_kernel(idx_ref, *refs, place):
    out_ref, scr = refs[4], refs[5]
    for k in range(4):
        scr[lax.rem(idx_ref[place] + 4 - k, 4)] = refs[k][...].astype(F32)
    out_ref[...] = ((scr[0] + scr[1]) + (scr[2] + scr[3])).astype(out_ref.dtype)


def ring_sum(idx, v, axis, place, dtype):
    pieces = [v] + [turn(v, axis, k) for k in range(1, 4)]
    return call(
        functools.partial(order_kernel, place=place), sds(v.shape, dtype), (idx, *pieces),
        [pltpu.VMEM((4,) + v.shape, F32)], 1, (0, 1_000_000), "ring",
    )


def per_device(
    inputs, norm_weight, gate_proj, inner_proj, state_proj, step_proj, inner_conv,
    inner_conv_bias, state_conv, state_conv_bias, step_bias, decay_log, skip_weight,
    gated_norm_weight, out_proj, segments, cotangent,
):
    x, cot = inputs[0], cotangent[0]
    core, y = lax.axis_index("core"), lax.axis_index("y")
    idx = jnp.stack([core, y, lax.axis_index("x"), lax.axis_index("z")]).astype(jnp.int32)
    row = lambda v: v.reshape(1, -1)
    nw = row(norm_weight)
    (normed, gate, inner, pre, mixed, dno, states, spre, raw, cols, scols, head, sums) = forward(
        x, cot, nw, gate_proj, inner_proj, state_proj, step_proj, inner_conv,
        row(inner_conv_bias), state_conv, row(state_conv_bias), row(step_bias), row(decay_log),
        row(skip_weight), row(gated_norm_weight), out_proj, segments,
    )
    tensor, dp = ("y", "core"), ("z", "x")
    sums = lax.all_to_all(jnp.broadcast_to(sums[None], (8, 2, T)), tensor, 0, 0, tiled=True)
    out_grad, gate_grad, no, gate_low, dy, gain = middle(
        sums, gate, mixed, dno, cols, cot, normed
    )
    out_grad = lax.psum(out_grad, dp)

    def dp_scatter(v):
        parts = lax.all_to_all(v.reshape(16, C // 16, D), dp, 0, 0, tiled=True)
        return jnp.sum(parts.astype(F32), axis=0).astype(BF)

    gate_part = dp_scatter(gate_grad)
    inner_grad, step_grad, inner_low, step_low, give, keep, small, heads = backward(
        idx, inner, pre, dy, spre, raw, cols, head, segments, normed
    )
    inner_part = dp_scatter(inner_grad)
    pieces = scatter(idx, give, keep)
    give, keep, pack = tail(
        idx, *pieces, states, spre, scols, segments, normed, gate_low, inner_low, step_low,
        gate_proj, inner_proj, step_proj, state_proj, step_grad, small, heads, gain,
    )
    pieces = scatter(idx, give, keep)
    start = core * GROUP + y * 64
    x_part = lax.dynamic_slice_in_dim(x, start, 64)
    cot_part = lax.dynamic_slice_in_dim(cot, start, 64)
    ig_part, norm_part = call(
        input_kernel, [sds((64, D), BF), sds((8, D), BF)], (*pieces, x_part, cot_part, nw), (), 0,
        (2_000_000, 1_000_000), "input_part",
    )
    pieces = scatter(idx, *product(idx, no, out_proj))
    out_part = call(
        output_kernel, sds((64, D), BF), (*pieces, x_part), (), 0, (1_000_000, 1_000_000), "out_part"
    )
    outputs = gather(idx, out_part, BF)
    input_grad = gather(idx, ig_part, F32)
    pack = jnp.concatenate([pack, norm_part], axis=0)
    pack = ring_sum(idx, ring_sum(idx, pack, "x", 2, BF), "z", 3, F32)
    ends = jnp.concatenate([pack[0:32], pack[40:48], pack[48:56]], axis=0).astype(BF)
    ends = gather(idx, ends, F32).reshape(8, 48, D)
    own = jnp.stack([gate_part, inner_part])
    whole = lax.all_to_all(
        jnp.broadcast_to(own[None], (16, 2, C // 16, D)), dp, 0, 0, tiled=True
    )
    gate_grad = whole[:, 0].reshape(C, D).T.astype(F32)
    inner_grad = whole[:, 1].reshape(C, D).T.astype(F32)
    state_grad = ends[:, 0:32].reshape(256, D).T
    state_small = ends[:, 32:40, C : C + 32].transpose(1, 0, 2).reshape(8, 256)
    norm_grad = jnp.sum(ends[:, 40], axis=0)
    return (
        outputs[None], input_grad[None], norm_grad, gate_grad, inner_grad, state_grad,
        pack[32 : 32 + NH].T, pack[40:44, 0:C], pack[44, 0:C], state_small[0:4], state_small[4],
        pack[40 : 40 + NH, 512], pack[40 : 40 + NH, 513], pack[40 : 40 + NH, 514], pack[45, 0:C],
        out_grad,
    )


def solution(mesh):
    small = Mesh(mesh.devices.reshape(4, 4, 4, 2), ("z", "x", "y", "core"))
    dp, tp = ("z", "x"), ("y", "core")
    placed = (
        P(dp, None, None), P(), P(None, tp), P(None, tp), P(), P(None, tp), P(None, tp), P(tp),
        P(), P(), P(tp), P(tp), P(tp), P(tp), P(tp, None), P(dp, None), P(dp, None, None),
    )
    out = (
        P(dp, None, None), P(dp, None, None), P(), P(None, tp), P(None, tp), P(), P(None, tp),
        P(None, tp), P(tp), P(), P(), P(tp), P(tp), P(tp), P(tp), P(tp, None),
    )
    return jax.shard_map(per_device, mesh=small, in_specs=placed, out_specs=out, check_vma=False)
```

```python
import functools

import jax
import jax.numpy as jnp
from jax import lax
from jax.experimental import pallas as pl
from jax.experimental.pallas import tpu as pltpu
from jax.sharding import Mesh, PartitionSpec as P

KERNEL = 4
INNER = 3072
EPS = 1e-05
T = 512
GROUP = 256
D = 1536
C = 384
NH = 6
HD = 64
N = 128
BF = jnp.bfloat16
F32 = jnp.float32
EXACT = lax.Precision.HIGHEST


def dot(a, b, precision=None):
    return jnp.dot(a, b, preferred_element_type=F32, precision=precision)


def dot_nt(a, b):
    return lax.dot_general(a, b, (((1,), (1,)), ((), ())), preferred_element_type=F32)


def dot_tn(a, b):
    return lax.dot_general(a, b, (((0,), (0,)), ((), ())), preferred_element_type=F32)


def sigmoid(v):
    return 1.0 / (1.0 + jnp.exp(-v))


def softplus(v):
    return jnp.maximum(v, 0.0) + jnp.log1p(jnp.exp(-jnp.abs(v)))


def lane_ids(rows, cols):
    return lax.broadcasted_iota(jnp.int32, (rows, cols), 1)


def row_ids(rows, cols):
    return lax.broadcasted_iota(jnp.int32, (rows, cols), 0)


def conv_masks(seg):
    lanes = lane_ids(1, T)
    out = []
    for k in range(1, KERNEL):
        same = (pltpu.roll(seg, k, 1) == seg) & (lanes >= k)
        out.append(same.astype(F32))
    return out


def conv_forward(v, cols, bias, masks):
    total = bias + cols[0] * v
    for k in range(1, KERNEL):
        total = total + cols[k] * (pltpu.roll(v, k, 1) * masks[k - 1])
    return total


def conv_backward(d_pre, v, cols, masks):
    d_v = cols[0] * d_pre
    taps = [jnp.sum(d_pre * v, axis=1, keepdims=True)]
    for k in range(1, KERNEL):
        back = pltpu.roll(d_pre * masks[k - 1], T - k, 1)
        d_v = d_v + cols[k] * back
        taps.append(jnp.sum(back * v, axis=1, keepdims=True))
    return d_v, taps, jnp.sum(d_pre, axis=1, keepdims=True)


def scan_logs(step, rate, rows_ref, segf):
    upper = (row_ids(GROUP, GROUP) <= lane_ids(GROUP, GROUP)).astype(F32)
    a = step * rate
    logs = jnp.concatenate(
        [dot(a[:, :GROUP], upper, EXACT), dot(a[:, GROUP:], upper, EXACT)], axis=1
    )
    rows_ref[...] = jnp.zeros_like(rows_ref)
    rows_ref[0:8, :] = logs
    rows_ref[8:9, :] = segf
    return logs, rows_ref[...].T


def link_mask(cols, segf, c):
    sl = slice(c * GROUP, (c + 1) * GROUP)
    same = cols[sl, 8:9] == segf[:, sl]
    later = lane_ids(GROUP, GROUP) >= row_ids(GROUP, GROUP)
    return jnp.where(same & later, 0.0, -1e30)


def state_rows(logs, segf):
    final = segf[:, GROUP - 1 : GROUP]
    tail = jnp.exp(logs[:, GROUP - 1 : GROUP] - logs[:, :GROUP]) * (
        segf[:, :GROUP] == final
    ).astype(F32)
    entry = jnp.exp(logs[:, GROUP:]) * (segf[:, GROUP:] == final).astype(F32)
    return tail, entry


def per_head(rows, width):
    return jnp.concatenate(
        [jnp.broadcast_to(rows[h : h + 1, :], (HD, width)) for h in range(NH)], axis=0
    )


class Source:
    def __init__(self, hbm, vmem, sem):
        self.copy, self.ref = pltpu.make_async_copy(hbm, vmem, sem), vmem
        self.copy.start()
        self.waits = True

    def __call__(self):
        if self.waits:
            self.copy.wait()
            self.waits = False
        return self.ref


class Target:
    def __init__(self, hbm, vmem, sem):
        self.copy, self.ref = pltpu.make_async_copy(vmem, hbm, sem), vmem
        self.sent = False

    def put(self):
        self.copy.start()
        self.sent = True


def sds(shape, dtype):
    return jax.ShapeDtypeStruct(shape, dtype)


class Here:
    def __init__(self, ref):
        self.ref = ref

    def __call__(self):
        return self.ref

    def put(self):
        pass


NEAR, FAR, FREE = pltpu.VMEM, pltpu.HBM, pl.ANY


def pinned(v, where):
    return v if where is FREE else pltpu.with_memory_space_constraint(v, where)


def call(
    body, outs, args, scratch=(), name=None, near=(), free=(), near_out=(), free_out=(), us=0.0,
    vmem=40,
):
    n, m = len(args) - 1, len(outs)
    where = [NEAR if k in near else FREE if k in free else FAR for k in range(n)]
    where_out = [NEAR if k in near_out else FREE if k in free_out else FAR for k in range(m)]
    far = [k for k in range(n) if k not in near]
    far_out = [k for k in range(m) if k not in near_out]

    def kernel(idx_ref, *refs):
        ins, results, rest = refs[:n], refs[n : n + m], refs[n + m :]
        buffers, rest = rest[: len(far)], rest[len(far) :]
        out_buffers, rest = rest[: len(far_out)], rest[len(far_out) :]
        in_sems, out_sems, *own = rest
        sources, targets = [Here(ref) for ref in ins], [Here(ref) for ref in results]
        for j, k in enumerate(far):
            sources[k] = Source(ins[k], buffers[j], in_sems.at[j])
        for j, k in enumerate(far_out):
            targets[k] = Target(results[k], out_buffers[j], out_sems.at[j])
        body(idx_ref, sources, targets, *own)
        for source in sources:
            source()
        for k in far_out:
            if not targets[k].sent:
                targets[k].put()
        for k in far_out:
            targets[k].copy.wait()

    buffers = [pltpu.VMEM(args[1 + k].shape, args[1 + k].dtype) for k in far]
    buffers += [pltpu.VMEM(outs[k].shape, outs[k].dtype) for k in far_out]
    sems = [pltpu.SemaphoreType.DMA((max(len(v), 1),)) for v in (far, far_out)]
    return launch(kernel, outs, args, [*buffers, *sems, *scratch], name, where, where_out, us, vmem)


def launch(kernel, outs, args, scratch, name, where, where_out, us=0.0, vmem=40):
    return pl.pallas_call(
        kernel,
        out_shape=[v if w is FREE else w(v.shape, v.dtype) for v, w in zip(outs, where_out)],
        in_specs=[pl.BlockSpec(memory_space=pltpu.SMEM)]
        + [pl.BlockSpec(memory_space=w) for w in where],
        out_specs=[pl.BlockSpec(memory_space=w) for w in where_out],
        scratch_shapes=scratch,
        compiler_params=pltpu.CompilerParams(vmem_limit_bytes=vmem << 20),
        cost_estimate=pl.CostEstimate(
            flops=int(us * 1e9) + 1000, bytes_accessed=1000, transcendentals=0
        ),
        name=name,
    )(args[0], *[pinned(v, w) for v, w in zip(args[1:], where)])


SPREAD_US, WIDEN_US, REDUCE_US, INPUT_US = 0.0, 20.0, 0.0, 20.0


def fwd_kernel(idx_ref, sources, targets, rows_scr, par_scr, u_scr, inner_scr):
    (
        x_in, nw_in, ic_in, icb_in, sc_in, scb_in, tb_in, dl_in, sk_in, gnw_in, seg_in, tp_in,
        ip_in, sp_in, gp_in, op_in, cot_in,
    ) = sources
    (
        normed_ref, gate_ref, inner_ref, pre_ref, mixed_ref, dno_ref, states_ref, spre_ref,
        raw_ref, cols_ref, scols_ref, head_ref, sums_ref, x_part_ref, cot_part_ref,
    ) = [target.ref for target in targets]
    par_scr[...] = jnp.zeros_like(par_scr)
    nw_ref, x_ref = nw_in(), x_in()

    def norm_block(r, _):
        sl = pl.ds(r * 64, 64)
        v = x_ref[sl, :].astype(F32)
        scale = lax.rsqrt(jnp.mean(v * v, axis=1, keepdims=True) + EPS)
        normed_ref[sl, :] = (v * scale * nw_ref[...].reshape(1, D)).astype(BF)
        return 0

    lax.fori_loop(0, T // 64, norm_block, 0)
    own = pl.ds(pl.multiple_of(idx_ref[0] * GROUP + idx_ref[1] * 64, 64), 64)
    x_part_ref[...] = x_ref[own, :]
    targets[0].put()
    targets[13].put()
    par_scr[0:4, 0:C] = ic_in()[...]
    par_scr[4:5, 0:C] = icb_in()[...].reshape(1, C)
    par_scr[5:6, 0:C] = gnw_in()[...].reshape(1, C)
    par_scr[0:4, C : C + 256] = sc_in()[...]
    par_scr[4:5, C : C + 256] = scb_in()[...].reshape(1, 256)
    par_scr[8:9, 0:NH] = tb_in()[...].reshape(1, NH)
    par_scr[9:10, 0:NH] = dl_in()[...].reshape(1, NH)
    par_scr[10:11, 0:NH] = sk_in()[...].reshape(1, NH)
    par = par_scr[...].T
    cols_ref[...] = par[0:C, 0:8]
    scols_ref[...] = par[C : C + 256, 0:8]
    head_ref[...] = par[0:8, :]
    normed = normed_ref[...]
    raw_ref[0:8, :] = jnp.concatenate(
        [dot_nt(tp_in()[...], normed), jnp.zeros((8 - NH, T), F32)], axis=0
    )
    segf = seg_in()[...].astype(F32)
    raw_ref[8:16, :] = jnp.broadcast_to(segf, (8, T))
    inner_scr[...] = dot(normed, ip_in()[...]).T
    inner_ref[...] = inner_scr[...].astype(BF)
    states = dot(normed, sp_in()[...]).T
    states_ref[...] = states.astype(BF)
    gate_ref[...] = dot(normed, gp_in()[...]).T
    for k in (1, 2, 6, 8, 9, 10, 11):
        targets[k].put()
    cot_ref = cot_in()
    dno_ref[...] = dot_nt(op_in()[...], cot_ref[...])
    cot_part_ref[...] = cot_ref[own, :]
    targets[5].put()
    targets[14].put()

    masks = conv_masks(segf)
    head = head_ref[...]
    step = softplus(raw_ref[0:8, :] + head[:, 8:9])
    rate = -jnp.exp(head[:, 9:10])
    logs, lcols = scan_logs(step, rate, rows_scr, segf)

    spre = conv_forward(
        states, [scols_ref[:, k : k + 1] for k in range(KERNEL)], scols_ref[:, 4:5], masks
    )
    spre_ref[...] = spre
    targets[7].put()
    cs = spre * sigmoid(spre)
    b_tok = cs[0:N, :].T.astype(BF)
    c_low = cs[N:, :].astype(BF)
    for h in range(NH):
        hs = slice(h * HD, (h + 1) * HD)
        pre = conv_forward(
            inner_scr[hs, :], [cols_ref[hs, k : k + 1] for k in range(KERNEL)],
            cols_ref[hs, 4:5], masks,
        )
        pre_ref[hs, :] = pre
        u_scr[hs, :] = pre * sigmoid(pre)
    targets[3].put()
    tail, entry = state_rows(logs, segf)
    weighted = u_scr[:, 0:GROUP] * per_head(step[:, 0:GROUP] * tail, GROUP)
    state = dot(weighted.astype(BF), b_tok[0:GROUP, :])
    entering = dot(state.astype(BF), c_low[:, GROUP:])
    for c in range(2):
        sl = slice(c * GROUP, (c + 1) * GROUP)
        neg = link_mask(lcols, segf, c)
        scores = dot(b_tok[sl, :], c_low[:, sl])
        for h in range(NH):
            hs = slice(h * HD, (h + 1) * HD)
            decay = jnp.exp((logs[h : h + 1, sl] - lcols[sl, h : h + 1]) + neg)
            m = (scores * decay).astype(BF)
            u = u_scr[hs, sl]
            y = dot((u * step[h : h + 1, sl]).astype(BF), m)
            if c == 1:
                y = y + entering[hs, :] * entry[h : h + 1, :]
            mixed_ref[hs, sl] = y + head[h : h + 1, 10:11] * u
    targets[4].put()
    squares = jnp.zeros((1, T), F32)
    dots = jnp.zeros((1, T), F32)
    for h in range(NH):
        hs = slice(h * HD, (h + 1) * HD)
        g = gate_ref[hs, :]
        gated = mixed_ref[hs, :] * (g * sigmoid(g))
        squares = squares + jnp.sum(gated * gated, axis=0, keepdims=True)
        dots = dots + jnp.sum(dno_ref[hs, :] * cols_ref[hs, 5:6] * gated, axis=0, keepdims=True)
    sums_ref[...] = jnp.broadcast_to(
        jnp.concatenate([squares, dots], axis=0)[None], sums_ref.shape
    )


def forward(*args):
    outs = [
        sds((T, D), BF), sds((C, T), F32), sds((C, T), BF), sds((C, T), F32), sds((C, T), F32),
        sds((C, T), F32), sds((256, T), BF), sds((256, T), F32), sds((16, T), F32),
        sds((C, 8), F32), sds((256, 8), F32), sds((8, 128), F32), sds((8, 2, T), F32),
        sds((64, D), BF), sds((64, D), BF),
    ]
    scratch = [
        pltpu.VMEM((128, T), F32), pltpu.VMEM((128, 640), F32), pltpu.VMEM((C, T), F32),
        pltpu.VMEM((C, T), F32),
    ]
    return call(fwd_kernel, outs, args, scratch, "forward", near_out=(1, 4, 5))


def mid_kernel(idx_ref, sources, targets, no_scr, low_scr):
    sums_in, gate_in, mixed_in, dno_in, cols_in, cot_in, normed_in = sources
    grads_ref, no_ref, gate_low_ref, dy_ref, gain_ref = [t.ref for t in targets]
    total = jnp.sum(sums_in()[...], axis=0)
    scale = lax.rsqrt(total[0:1, :] / INNER + EPS)
    slope = scale * scale * scale * (total[1:2, :] / INNER)
    gate_ref, mixed_ref, dno_ref, cols_ref = gate_in(), mixed_in(), dno_in(), cols_in()
    for h in range(NH):
        hs = slice(h * HD, (h + 1) * HD)
        g = gate_ref[hs, :]
        s = sigmoid(g)
        silu = g * s
        mixed = mixed_ref[hs, :]
        gated = mixed * silu
        gain = cols_ref[hs, 5:6]
        normal = gated * scale
        no_scr[hs, :] = (normal * gain).astype(BF)
        dno = dno_ref[hs, :]
        gain_ref[hs, :] = jnp.broadcast_to(jnp.sum(dno * normal, axis=1, keepdims=True), (HD, 8))
        d_gated = scale * (dno * gain) - gated * slope
        low_scr[hs, :] = (d_gated * mixed * (s * (1.0 + g * (1.0 - s)))).astype(BF)
        dy_ref[hs, :] = (d_gated * silu).astype(BF)
    targets[3].put()
    out_grad = dot(no_scr[...], cot_in()[...]).astype(BF)
    for k in range(16):
        rows, columns = slice(k % 4 * 96, (k % 4 + 1) * 96), slice(k // 4 * C, (k // 4 + 1) * C)
        grads_ref[k, 96:192, :] = out_grad[rows, columns]
    gate_grad = dot(low_scr[...], normed_in()[...]).T.astype(BF)
    for k in range(16):
        grads_ref[k, 0:96, :] = gate_grad[k * 96 : (k + 1) * 96, :]
    targets[0].put()
    no_ref[...] = no_scr[...].T
    gate_low_ref[...] = low_scr[...].T


def middle(*args):
    outs = [
        sds((16, 192, C), BF), sds((T, C), BF), sds((T, C), BF), sds((C, T), BF), sds((C, 8), F32),
    ]
    scratch = [pltpu.VMEM((C, T), BF), pltpu.VMEM((C, T), BF)]
    return call(mid_kernel, outs, args, scratch, "middle", near=(1, 2, 3), free=(0,))


def bwd_kernel(
    idx_ref, sources, targets, rows_scr, u_scr, di_scr, low_scr, cs_scr, slow_scr, tpad, pad_scr,
    grad_scr, tok_scr, low_tok, step_tok, give_scr,
):
    (
        raw_in, head_in, spre_in, pre_in, dy_in, cols_in, inner_in, normed_in, scols_in,
        states_in, gate_low_in, sp_in, tp_in, gp_in, ip_in, no_in, op_in,
    ) = sources
    inner_grad_ref, keep_ref, extra_ref, *gives = [t.ref for t in targets]
    core = idx_ref[0]
    raw_ref, head_ref, spre_ref = raw_in(), head_in(), spre_in()
    segf = raw_ref[8:9, :]
    masks = conv_masks(segf)
    head = head_ref[...]
    raw = raw_ref[0:8, :] + head[:, 8:9]
    step = softplus(raw)
    rate = -jnp.exp(head[:, 9:10])
    logs, lcols = scan_logs(step, rate, rows_scr, segf)
    spre = spre_ref[...]
    cs = spre * sigmoid(spre)
    b_low = cs[0:N, :].astype(BF)
    c_low = cs[N:, :].astype(BF)
    b_tok = cs[0:N, :].T.astype(BF)
    c_tok = cs[N:, :].T.astype(BF)
    pre_ref, dy_ref = pre_in(), dy_in()
    for h in range(NH):
        hs = slice(h * HD, (h + 1) * HD)
        pre = pre_ref[hs, :]
        u_scr[hs, :] = pre * sigmoid(pre)
    tail, entry = state_rows(logs, segf)
    first, second = slice(0, GROUP), slice(GROUP, T)
    weighted = (u_scr[:, first] * per_head(step[:, first] * tail, GROUP)).astype(BF)
    state = dot(weighted, b_tok[first, :]).astype(BF)
    d_entering = (dy_ref[:, second] * per_head(entry, GROUP)).astype(BF)
    d_state = dot(d_entering, c_tok[second, :]).astype(BF)
    entering = dot(state, c_low[:, second])
    into = dot(d_state, b_low[:, first])
    d_c_second = dot_tn(state, d_entering)
    d_b_first = dot_tn(d_state, weighted)
    tri = (row_ids(GROUP, GROUP) >= lane_ids(GROUP, GROUP)).astype(BF)
    before = (row_ids(GROUP, GROUP) < lane_ids(GROUP, GROUP)).astype(F32)
    upto = (row_ids(GROUP, GROUP) < lane_ids(GROUP, GROUP)).astype(F32)
    since = (row_ids(GROUP, GROUP) >= lane_ids(GROUP, GROUP)).astype(F32)
    out_step = []
    out_skip = []
    da_rows = [[None, None] for _ in range(NH)]
    for c in range(2):
        sl = slice(c * GROUP, (c + 1) * GROUP)
        neg = link_mask(lcols, segf, c)
        scores = dot(b_tok[sl, :], c_low[:, sl])
        d_scores = jnp.zeros((GROUP, GROUP), F32)
        for h in range(NH):
            hs = slice(h * HD, (h + 1) * HD)
            decay = jnp.exp((logs[h : h + 1, sl] - lcols[sl, h : h + 1]) + neg)
            m = scores * decay
            dy = dy_ref[hs, sl]
            inflow = (u_scr[hs, sl] * step[h : h + 1, sl]).astype(BF)
            g = dot_tn(inflow, dy)
            d_scores = d_scores + g * decay
            w = dot((g * m).astype(BF), tri)
            da = jnp.sum(w * before, axis=0, keepdims=True)
            da_rows[h][c] = da
            di = dot_nt(dy, m.astype(BF))
            if c == 0:
                di = di + into[hs, :] * tail[h : h + 1, :]
            di_scr[hs, sl] = di
        ds = d_scores.astype(BF)
        d_b = dot_nt(c_low[:, sl], ds)
        d_c = dot(b_low[:, sl], ds)
        if c == 0:
            d_b = d_b + d_b_first
        else:
            d_c = d_c + d_c_second
        cs_scr[0:N, sl] = d_b
        cs_scr[N:, sl] = d_c
    cols_ref, inner_ref, normed_ref = cols_in(), inner_in(), normed_in()
    zero = jnp.zeros((1, GROUP), F32)
    q_rows, e_rows = [], []
    for h in range(NH):
        hs = slice(h * HD, (h + 1) * HD)
        q = u_scr[hs, first] * step[h : h + 1, first] * into[hs, :]
        q_rows.append(jnp.sum(q, axis=0, keepdims=True))
        e = dy_ref[hs, second] * entering[hs, :]
        e_rows.append(jnp.sum(e, axis=0, keepdims=True))
    q8 = jnp.concatenate(q_rows + [zero, zero], axis=0) * tail
    e8 = jnp.concatenate(e_rows + [zero, zero], axis=0) * entry
    da0 = jnp.concatenate([da_rows[h][0] for h in range(NH)] + [zero, zero], axis=0)
    da1 = jnp.concatenate([da_rows[h][1] for h in range(NH)] + [zero, zero], axis=0)
    da = jnp.concatenate([da0 + dot(q8, upto, EXACT), da1 + dot(e8, since, EXACT)], axis=1)
    d_steps = []
    pad_scr[...] = jnp.zeros_like(pad_scr)
    for h in range(NH):
        hs = slice(h * HD, (h + 1) * HD)
        pre = pre_ref[hs, :]
        s = sigmoid(pre)
        u = u_scr[hs, :]
        di = di_scr[hs, :]
        dy = dy_ref[hs, :].astype(F32)
        d_steps.append(jnp.sum(di * u, axis=0, keepdims=True))
        out_skip.append(jnp.sum(dy * u, axis=0, keepdims=True))
        d_u = di * step[h : h + 1, :] + head[h : h + 1, 10:11] * dy
        d_pre = d_u * (s * (1.0 + pre * (1.0 - s)))
        d_v, taps, bias = conv_backward(
            d_pre, inner_ref[hs, :].astype(F32),
            [cols_ref[hs, k : k + 1] for k in range(KERNEL)], masks,
        )
        low_scr[hs, :] = d_v.astype(BF)
        for k in range(KERNEL):
            pad_scr[hs, k : k + 1] = taps[k]
        pad_scr[hs, 4:5] = bias
    zero = jnp.zeros((2, T), F32)
    d_step = jnp.concatenate(d_steps + [zero], axis=0) + da * rate
    skips = jnp.concatenate(out_skip + [zero], axis=0)
    d_raw = d_step * sigmoid(raw)
    inner_grad_ref[...] = dot(low_scr[...], normed_ref[...]).T.astype(BF)
    targets[0].put()
    rows_scr[...] = jnp.zeros_like(rows_scr)
    rows_scr[0:8, :] = d_raw
    step_tok[...] = rows_scr[...].T.astype(BF)
    extra_ref[0:8, :] = dot(d_raw.astype(BF), normed_ref[...])
    scols_ref, states_ref = scols_in(), states_in()
    for part in range(4):
        rs = slice(part * 64, (part + 1) * 64)
        ps = slice(C + part * 64, C + (part + 1) * 64)
        pre = spre_ref[rs, :]
        s = sigmoid(pre)
        d_pre = cs_scr[rs, :] * (s * (1.0 + pre * (1.0 - s)))
        d_v, taps, bias = conv_backward(
            d_pre, states_ref[rs, :].astype(F32),
            [scols_ref[rs, k : k + 1] for k in range(KERNEL)], masks,
        )
        slow_scr[rs, :] = d_v.astype(BF)
        for k in range(KERNEL):
            pad_scr[ps, k : k + 1] = taps[k]
        pad_scr[ps, 4:5] = bias
    rows = pad_scr[...].T[0:8, :]
    columns = [
        jnp.sum(d_raw, axis=1, keepdims=True), jnp.sum(da * step, axis=1, keepdims=True) * rate,
        jnp.sum(skips, axis=1, keepdims=True), jnp.zeros((8, 125), F32),
    ]
    extra_ref[8:16, :] = jnp.concatenate(
        [rows[:, 0:C], *columns, jnp.zeros((8, D - C - 128), F32)], axis=1
    )
    targets[2].put()
    taps = jnp.concatenate(
        [
            jnp.concatenate([rows[:, C:], jnp.zeros((8, D - 256), F32)], axis=1),
            jnp.zeros((8, D), F32),
        ],
        axis=0,
    ).astype(BF)
    tok_scr[...] = slow_scr[...].T
    low_tok[...] = low_scr[...].T
    grad_scr[...] = dot(slow_scr[...], normed_ref[...]).astype(BF)
    tpad[...] = jnp.zeros_like(tpad)
    tpad[0:NH, :] = tp_in()[...]
    gate_low_ref, no_ref = gate_low_in(), no_in()
    gp_ref, ip_ref, sp_ref, op_ref = gp_in(), ip_in(), sp_in(), op_in()
    for give, half in ((True, 1 - core), (False, core)):
        tok = pl.ds(pl.multiple_of(half * GROUP, GROUP), GROUP)
        total = dot_nt(gate_low_ref[tok, :], gp_ref[...])
        total = total + dot_nt(low_tok[tok, :], ip_ref[...])
        total = total + dot_nt(tok_scr[tok, :], sp_ref[...])
        total = (total + dot(step_tok[tok, :], tpad[...])).astype(BF)
        out = dot(no_ref[tok, :], op_ref[...]).astype(BF)
        for k in range(4):
            slot = lax.rem(k + 4 - idx_ref[1], 4)
            rows = pl.ds(pl.multiple_of(half * 128 + k * 32, 32), 32)
            ref = give_scr if give else keep_ref
            ref[slot, 0:64, :] = total[k * 64 : (k + 1) * 64, :]
            ref[slot, 64:96, :] = grad_scr[rows, :]
            ref[slot, 96:112, :] = taps
            ref[slot, 112:176, :] = out[k * 64 : (k + 1) * 64, :]
        if give:
            for k in range(4):
                gives[k][...] = give_scr[k]


def backward(*args):
    outs = [sds((D, C), BF), sds((4, 176, D), BF), sds((16, D), F32), *[sds((176, D), BF)] * 4]
    scratch = [
        pltpu.VMEM((128, T), F32), pltpu.VMEM((C, T), F32), pltpu.VMEM((C, T), F32),
        pltpu.VMEM((C, T), BF), pltpu.VMEM((256, T), F32), pltpu.VMEM((256, T), BF),
        pltpu.VMEM((128, D), BF), pltpu.VMEM((C + 256, 128), F32), pltpu.VMEM((256, D), BF),
        pltpu.VMEM((T, 256), BF), pltpu.VMEM((T, C), BF), pltpu.VMEM((T, 128), BF),
        pltpu.VMEM((4, 176, D), BF),
    ]
    return call(bwd_kernel, outs, args, scratch, "backward", near_out=(1, 3, 4, 5, 6))


def fold_kernel(idx_ref, keep, g0, g1, g2, g3, own_hbm, s1, s2, s3, own, sem):
    for k in (0, 1, 2, 3):
        total = keep[k].astype(F32) + (g0, g1, g2, g3)[k][...].astype(F32)
        if k == 0:
            own[...] = total
            store = pltpu.make_async_copy(own, own_hbm, sem)
            store.start()
        else:
            (s1, s2, s3)[k - 1][...] = total.astype(BF)
    store.wait()


def swap(v):
    return lax.ppermute(v, "core", [(0, 1), (1, 0)])


def turn(v, axis, by):
    return lax.ppermute(v, axis, [(i, (i + by) % 4) for i in range(4)])


def scatter(idx, gives, keep):
    _, rows, width = keep.shape
    outs = [sds((rows, width), F32)] + [sds((rows, width), BF)] * 3
    scratch = [pltpu.VMEM((rows, width), F32), pltpu.SemaphoreType.DMA(())]
    own, *sends = launch(
        fold_kernel, outs, (idx, keep, *map(swap, gives)), scratch, "fold", [NEAR] * 5,
        [FAR, NEAR, NEAR, NEAR], vmem=16,
    )
    return [own] + [turn(send, "y", k + 1) for k, send in enumerate(sends)]


def gather(chunk, *earlier):
    pieces = [chunk] + [turn(chunk, "y", k) for k in range(1, 4)]
    return pieces + [swap(after(piece, *earlier)) for piece in pieces]


def place_of(idx_ref, k):
    half = idx_ref[0] if k < 4 else 1 - idx_ref[0]
    return half, half * 4 + lax.rem(idx_ref[1] + 4 - k % 4, 4)


def finish_kernel(idx_ref, *refs):
    pieces, out_hbm, grad_hbm = refs[:8], refs[8], refs[9]
    buf, grad, in_sems, out_sems = refs[10:]
    loads = [pltpu.make_async_copy(pieces[k], buf.at[k], in_sems.at[k]) for k in range(8)]
    for load in loads:
        load.start()
    stores = []
    for k in range(8):
        _, place = place_of(idx_ref, k)
        rows = pl.ds(pl.multiple_of(place * 64, 64), 64)
        loads[k].wait()
        stores.append(
            pltpu.make_async_copy(buf.at[k, 64:128], out_hbm.at[rows], out_sems.at[0, k])
        )
        stores[-1].start()
        grad[k] = buf[k, 0:64, :].astype(F32)
        stores.append(pltpu.make_async_copy(grad.at[k], grad_hbm.at[rows], out_sems.at[1, k]))
        stores[-1].start()
    for store in stores:
        store.wait()


def ends_kernel(idx_ref, sources, targets, state_scr, small_scr):
    (
        state_ref, norm_ref, sconv_ref, sbias_ref, step_ref, taps_ref, bias_ref, tb_ref, dl_ref,
        sk_ref, gnw_ref,
    ) = [t.ref for t in targets]
    for k in range(8):
        _, place = place_of(idx_ref, k)
        piece = sources[k]()
        for j in range(4):
            columns = slice(j * C, (j + 1) * C)
            for half in range(2):
                rows = pl.ds(pl.multiple_of(place * 32 + half * 16, 16), 16)
                state_scr[rows, columns] = piece[j * 4 + half].astype(F32)
            small_scr[place, :, columns] = piece[j * 4 + 2].astype(F32)
    for row in range(12):
        sl = slice(row * 128, (row + 1) * 128)
        state_ref[sl, :] = state_scr[:, sl].T
    targets[0].put()
    sconv_ref[...] = small_scr[0, 0:4, 0:256]
    sbias_ref[...] = small_scr[0, 4:5, 0:256].reshape(256)
    norm = small_scr[0, 8:9, :]
    for k in range(1, 8):
        norm = norm + small_scr[k, 8:9, :]
    norm_ref[...] = norm.reshape(D)
    own = sources[0]()
    for j in range(4):
        step_ref[:, j * C : (j + 1) * C] = own[j * 4 + 3][0:NH, :].astype(F32)
    smalls = jnp.concatenate([own[3], own[7]], axis=1)[8:16, :].astype(F32)
    taps_ref[...] = smalls[0:4, 0:C]
    bias_ref[...] = smalls[4:5, 0:C].reshape(C)
    gnw_ref[...] = smalls[5:6, 0:C].reshape(C)
    heads = jnp.concatenate([smalls[:, C : C + 128], jnp.zeros((120, 128), F32)], axis=0).T
    tb_ref[...] = heads[0:1, 0:NH].reshape(NH)
    dl_ref[...] = heads[1:2, 0:NH].reshape(NH)
    sk_ref[...] = heads[2:3, 0:NH].reshape(NH)


def input_kernel(idx_ref, sources, targets, pad_scr):
    x_ref, cot_ref, nw_ref, extra_ref, gain_ref = [source() for source in sources[:5]]
    chunk_ref, pack_ref = [t.ref for t in targets]
    p0, p1, p2, p3 = [source() for source in sources[5:]]
    total = (p0[...] + p1[...].astype(F32)) + (p2[...].astype(F32) + p3[...].astype(F32))
    d_normed = total[0:64, :]
    v = x_ref[...].astype(F32)
    scale = lax.rsqrt(jnp.mean(v * v, axis=1, keepdims=True) + EPS)
    weighted = d_normed * nw_ref[...].reshape(1, D)
    grad = scale * weighted - v * (
        scale * scale * scale * jnp.mean(weighted * v, axis=1, keepdims=True)
    )
    chunk_ref[0:64, :] = (cot_ref[...].astype(F32) + grad).astype(BF)
    chunk_ref[64:128, :] = (v + total[112:176, :]).astype(BF)
    targets[0].put()
    norm = jnp.broadcast_to(jnp.sum(d_normed * v * scale, axis=0, keepdims=True), (8, D))
    pad_scr[...] = jnp.zeros_like(pad_scr)
    pad_scr[:, 5:6] = gain_ref[:, 0:1]
    gain = jnp.concatenate([pad_scr[...].T[0:8, :], jnp.zeros((8, D - C), F32)], axis=1)
    rows = [
        total[64:80, :], total[80:96, :], jnp.concatenate([total[96:104, :], norm], axis=0),
        jnp.concatenate([extra_ref[0:8, :], extra_ref[8:16, :] + gain], axis=0),
    ]
    for k in range(16):
        pack_ref[k] = rows[k % 4][:, k // 4 * C : (k // 4 + 1) * C].astype(BF)


def share_kernel(idx_ref, sources, targets):
    total = total_of(sources[0]())
    for k in range(16):
        targets[0].ref[k] = total


def total_of(parts_ref):
    total = parts_ref[0].astype(F32)
    for k in range(1, 16):
        total = total + parts_ref[k].astype(F32)
    return total.astype(BF)


def reduce_kernel(idx_ref, sources, targets):
    targets[0].ref[...] = total_of(sources[0]())


def spread_kernel(idx_ref, parts_hbm, out_hbm, parts, own, sem, sems):
    load = pltpu.make_async_copy(parts_hbm, parts, sem)
    load.start()
    load.wait()
    own[...] = total_of(parts)
    stores = [pltpu.make_async_copy(own, out_hbm.at[k], sems.at[k]) for k in range(16)]
    for store in stores:
        store.start()
    for store in stores:
        store.wait()


def widen_kernel(idx_ref, hbm, wide_hbm, buf, wide, in_sems, out_sems):
    loads = [pltpu.make_async_copy(hbm.at[k], buf.at[k], in_sems.at[k]) for k in range(4)]
    for load in loads:
        load.start()
    stores = []
    for k in range(4):
        loads[k].wait()
        wide[k] = buf[k].astype(F32)
        stores.append(pltpu.make_async_copy(wide.at[k], wide_hbm.at[k], out_sems.at[k]))
        stores[-1].start()
    for store in stores:
        store.wait()


def widen_two_kernel(idx_ref, hbm, out_hbm, gate_hbm, buf, out, gate, in_sems, out_sems):
    loads = [pltpu.make_async_copy(hbm.at[k], buf.at[k], in_sems.at[k]) for k in range(4)]
    for load in loads:
        load.start()
    stores = []
    for k in range(4):
        loads[k].wait()
        for j in range(4):
            gate[k, j] = buf[k, j, 0:96, :].astype(F32)
            out[k, j * 96 : (j + 1) * 96, :] = buf[k, j, 96:192, :].astype(F32)
        columns = slice(k * C, (k + 1) * C)
        stores.append(pltpu.make_async_copy(gate.at[k], gate_hbm.at[k], out_sems.at[0, k]))
        stores.append(
            pltpu.make_async_copy(out.at[k], out_hbm.at[:, columns], out_sems.at[1, k])
        )
        stores[-2].start()
        stores[-1].start()
    for store in stores:
        store.wait()


def after(idx, *values):
    return lax.optimization_barrier((idx, *values))[0]


def per_device(
    inputs, norm_weight, gate_proj, inner_proj, state_proj, step_proj, inner_conv,
    inner_conv_bias, state_conv, state_conv_bias, step_bias, decay_log, skip_weight,
    gated_norm_weight, out_proj, segments, cotangent,
):
    x, cot, step_rows = inputs[0], cotangent[0], step_proj.T
    dma = pltpu.SemaphoreType.DMA
    idx = jnp.stack([lax.axis_index(a) for a in ("core", "y", "x", "z")]).astype(jnp.int32)
    (
        normed, gate, inner, pre, mixed, dno, states, spre, raw, cols, scols, head, sums, x_part,
        cot_part,
    ) = forward(
        idx, x, norm_weight, inner_conv, inner_conv_bias, state_conv, state_conv_bias, step_bias,
        decay_log, skip_weight, gated_norm_weight, segments, step_rows, inner_proj, state_proj,
        gate_proj, out_proj, cot,
    )
    sums = lax.all_to_all(sums, ("y", "core"), 0, 0, tiled=True)
    grads, no, gate_low, dy, gain = middle(idx, sums, gate, mixed, dno, cols, cot, normed)

    def dp_terms(v):
        return lax.all_to_all(v, ("x", "z"), 0, 0, tiled=True)

    first_terms = dp_terms(grads)
    inner_grad, keep, extra, *gives = backward(
        idx, raw, head, spre, pre, dy, cols, inner, normed, scols, states, gate_low, state_proj,
        step_rows, gate_proj, inner_proj, no, out_proj,
    )
    pieces = scatter(idx, gives, keep)
    (first,) = call(
        reduce_kernel, [sds((192, C), BF)], (after(idx, pieces[0]), first_terms), name="reduce",
        free=(0,), us=REDUCE_US,
    )
    inner_grad = after(inner_grad.reshape(16, D // 16, C), first)
    inner_terms = dp_terms(inner_grad)
    first = lax.all_gather(first, ("x", "z"))
    chunk, pack = call(
        input_kernel, [sds((128, D), BF), sds((16, 16, C), BF)],
        (idx, x_part, cot_part, norm_weight, extra, gain, *pieces),
        [pltpu.VMEM((C, 128), F32)], "input_part", free=(6, 7, 8), free_out=(0, 1),
        us=INPUT_US,
    )
    (spread,) = launch(
        spread_kernel, [sds((16, D // 16, C), BF)], (after(idx, chunk), inner_terms),
        [
            pltpu.VMEM((16, D // 16, C), BF), pltpu.VMEM((D // 16, C), BF), dma(()), dma((16,)),
        ],
        "spread", [FREE], [FAR], SPREAD_US,
    )
    (pack,) = call(
        share_kernel, [sds((16, 16, C), BF)], (idx, dp_terms(after(pack, spread))), name="share",
        free=(0,), free_out=(0,),
    )
    parts = gather(chunk, pack)
    outputs, input_grad = launch(
        finish_kernel, [sds((T, D), BF), sds((T, D), F32)], (idx, *parts),
        [
            pltpu.VMEM((8, 128, D), BF), pltpu.VMEM((8, 64, D), F32), dma((8,)), dma((2, 8)),
        ],
        "finish", [FREE] * 8, [FAR] * 2,
    )
    pack = dp_terms(pack)
    whole = dp_terms(after(spread, pack, input_grad))
    (
        state_grad, norm_grad, sconv, sbias, step_grad, taps, bias, tb, dl, sk, gnw,
    ) = call(
        ends_kernel,
        [
            sds((D, 256), F32), sds((D,), F32), sds((KERNEL, 256), F32), sds((256,), F32),
            sds((NH, D), F32), sds((KERNEL, C), F32), sds((C,), F32), sds((NH,), F32),
            sds((NH,), F32), sds((NH,), F32), sds((C,), F32),
        ],
        (idx, *gather(pack)), [pltpu.VMEM((256, D), F32), pltpu.VMEM((8, 16, D), F32)], "ends",
        free=range(8),
    )
    (inner_grad,) = launch(
        widen_kernel, [sds((4, 384, C), F32)], (idx, whole.reshape(4, 384, C)),
        [pltpu.VMEM((4, 384, C), BF), pltpu.VMEM((4, 384, C), F32), dma((4,)), dma((4,))],
        "widen", [FREE], [FAR], WIDEN_US,
    )
    out_grad, gate_grad = launch(
        widen_two_kernel, [sds((C, D), F32), sds((4, 4, 96, C), F32)],
        (idx, first.reshape(4, 4, 192, C)),
        [
            pltpu.VMEM((4, 4, 192, C), BF), pltpu.VMEM((4, C, C), F32),
            pltpu.VMEM((4, 4, 96, C), F32), dma((4,)), dma((2, 4)),
        ],
        "widen_two", [FAR], [FAR] * 2,
    )
    return (
        outputs[None], input_grad[None], norm_grad, gate_grad.reshape(D, C),
        inner_grad.reshape(D, C), state_grad, step_grad.T, taps, bias, sconv, sbias, tb, dl, sk,
        gnw, out_grad,
    )


def solution(mesh):
    small = Mesh(mesh.devices.reshape(4, 4, 4, 2), ("z", "x", "y", "core"))
    dp, tp = ("z", "x"), ("y", "core")
    placed = (
        P(dp, None, None), P(), P(None, tp), P(None, tp), P(), P(None, tp), P(None, tp), P(tp),
        P(), P(), P(tp), P(tp), P(tp), P(tp), P(tp, None), P(dp, None), P(dp, None, None),
    )
    out = (
        P(dp, None, None), P(dp, None, None), P(), P(None, tp), P(None, tp), P(), P(None, tp),
        P(None, tp), P(tp), P(), P(), P(tp), P(tp), P(tp), P(tp), P(tp, None),
    )
    return jax.shard_map(per_device, mesh=small, in_specs=placed, out_specs=out, check_vma=False)
```

```python
import functools

import jax
import jax.numpy as jnp
from jax import lax
from jax.experimental import pallas as pl
from jax.experimental.pallas import tpu as pltpu
from jax.sharding import Mesh, PartitionSpec as P

KERNEL = 4
INNER = 3072
EPS = 1e-05
T = 512
GROUP = 256
D = 1536
C = 384
NH = 6
HD = 64
N = 128
BF = jnp.bfloat16
F32 = jnp.float32
EXACT = lax.Precision.HIGHEST


def dot(a, b, precision=None):
    return jnp.dot(a, b, preferred_element_type=F32, precision=precision)


def dot_nt(a, b):
    return lax.dot_general(a, b, (((1,), (1,)), ((), ())), preferred_element_type=F32)


def dot_tt(a, b):
    return lax.dot_general(a, b, (((0,), (1,)), ((), ())), preferred_element_type=F32)


def dot_tn(a, b):
    return lax.dot_general(a, b, (((0,), (0,)), ((), ())), preferred_element_type=F32)


def sigmoid(v):
    return 1.0 / (1.0 + jnp.exp(-v))


def softplus(v):
    return jnp.maximum(v, 0.0) + jnp.log1p(jnp.exp(-jnp.abs(v)))


def lane_ids(rows, cols):
    return lax.broadcasted_iota(jnp.int32, (rows, cols), 1)


def row_ids(rows, cols):
    return lax.broadcasted_iota(jnp.int32, (rows, cols), 0)


def conv_masks(seg):
    lanes = lane_ids(1, T)
    out = []
    for k in range(1, KERNEL):
        same = (pltpu.roll(seg, k, 1) == seg) & (lanes >= k)
        out.append(same.astype(F32))
    return out


def conv_forward(v, cols, bias, masks):
    total = bias + cols[0] * v
    for k in range(1, KERNEL):
        total = total + cols[k] * (pltpu.roll(v, k, 1) * masks[k - 1])
    return total


def conv_backward(dp_scr, v_ref, taps_ref, mark_scr, out_ref):
    width = v_ref.shape[1]
    rows = 32
    taps = [jnp.zeros((8, width), F32) for _ in range(KERNEL + 1)]

    def fold(v):
        return jnp.sum(v.reshape(rows // 8, 8, width), axis=0)

    for first in range(0, T, rows):
        here = slice(first, first + rows)
        v = v_ref[here, :].astype(F32)
        d_pre = dp_scr[here, :]
        total = taps_ref[0:1, :] * d_pre
        taps[0] = taps[0] + fold(d_pre * v)
        taps[KERNEL] = taps[KERNEL] + fold(d_pre)
        for k in range(1, KERNEL):
            mark = jnp.concatenate([mark_scr[k - 1, here, :]] * (width // 128), axis=1)
            back = dp_scr[first + k : first + k + rows, :] * mark
            total = total + taps_ref[k : k + 1, :] * back
            taps[k] = taps[k] + fold(back * v)
        out_ref[here, :] = total.astype(BF)
    sums = [jnp.sum(tap, axis=0, keepdims=True) for tap in taps]
    return jnp.concatenate([*sums, jnp.zeros((3, width), F32)], axis=0)


def scan_logs(step, rate, rows_ref, segf, more=()):
    upper = (row_ids(GROUP, GROUP) <= lane_ids(GROUP, GROUP)).astype(F32)
    a = step * rate
    logs = jnp.concatenate(
        [dot(a[:, :GROUP], upper, EXACT), dot(a[:, GROUP:], upper, EXACT)], axis=1
    )
    rows_ref[...] = jnp.zeros_like(rows_ref)
    rows_ref[0:8, :] = logs
    rows_ref[8:9, :] = segf
    for k, row in enumerate(more):
        rows_ref[9 + k : 10 + k, :] = row
    return logs, rows_ref[...].T


def link_mask(cols, segf, c):
    sl = slice(c * GROUP, (c + 1) * GROUP)
    same = cols[sl, 8:9] == segf[:, sl]
    later = lane_ids(GROUP, GROUP) >= row_ids(GROUP, GROUP)
    return jnp.where(same & later, 0.0, -1e30)


def state_rows(logs, segf):
    final = segf[:, GROUP - 1 : GROUP]
    tail = jnp.exp(logs[:, GROUP - 1 : GROUP] - logs[:, :GROUP]) * (
        segf[:, :GROUP] == final
    ).astype(F32)
    entry = jnp.exp(logs[:, GROUP:]) * (segf[:, GROUP:] == final).astype(F32)
    return tail, entry


def per_head(rows, width):
    return jnp.concatenate(
        [jnp.broadcast_to(rows[h : h + 1, :], (HD, width)) for h in range(NH)], axis=0
    )


class Source:
    def __init__(self, hbm, vmem, sem):
        self.ref, self.waits = vmem, True
        if isinstance(sem, list):
            rows = vmem.shape[0] // len(sem)
            parts = [slice(k * rows, (k + 1) * rows) for k in range(len(sem))]
            self.copies = [
                pltpu.make_async_copy(hbm.at[part], vmem.at[part], one)
                for part, one in zip(parts, sem)
            ]
        else:
            self.copies = [pltpu.make_async_copy(hbm, vmem, sem)]
        for copy in self.copies:
            copy.start()

    def __call__(self):
        if self.waits:
            for copy in self.copies:
                copy.wait()
            self.waits = False
        return self.ref


class Target:
    def __init__(self, hbm, vmem, sem):
        self.hbm, self.ref, self.sem = hbm, vmem, sem
        self.copies = []

    def put(self):
        self.copies.append(pltpu.make_async_copy(self.ref, self.hbm, self.sem))
        self.copies[-1].start()


def sds(shape, dtype):
    return jax.ShapeDtypeStruct(shape, dtype)


class Here:
    def __init__(self, ref):
        self.ref = ref

    def __call__(self):
        return self.ref

    def put(self):
        pass


NEAR, FAR, FREE = pltpu.VMEM, pltpu.HBM, pl.ANY


def pinned(v, where):
    return v if where is FREE else pltpu.with_memory_space_constraint(v, where)


def call(
    body, outs, args, scratch=(), name=None, near=(), free=(), near_out=(), free_out=(), us=0.0,
    vmem=40, into=None, twin=None, split=None,
):
    into, twin = into or {}, twin or {}
    n, m = len(args) - 1, len(outs)
    where = [NEAR if k in near else FREE if k in free else FAR for k in range(n)]
    where_out = [NEAR if k in near_out else FREE if k in free_out else FAR for k in range(m)]
    far = [k for k in range(n) if k not in near]
    far_out = [k for k in range(m) if k not in near_out]

    def kernel(idx_ref, *refs):
        ins, results, rest = refs[:n], refs[n : n + m], refs[n + m :]
        *buffers, in_sems, out_sems = rest[: count + 2]
        own = rest[count + 2 :]
        sources, targets = [Here(ref) for ref in ins], [Here(ref) for ref in results]
        for j, k in enumerate(far):
            buffer = results[into[k]] if k in into else buffers.pop(0)
            sem = in_sems.at[j]
            if k == split:
                sem = [sem, *[in_sems.at[len(far) + i] for i in range(3)]]
            sources[k] = Source(ins[k], buffer, sem)
        for j, k in enumerate(far_out):
            buffer = results[twin[k]] if k in twin else buffers.pop(0)
            targets[k] = Target(results[k], buffer, out_sems.at[j])
        body(idx_ref, sources, targets, *own)
        for source in sources:
            source()
        for k in far_out:
            if not targets[k].copies:
                targets[k].put()
        for k in far_out:
            for copy in targets[k].copies:
                copy.wait()

    buffers = [pltpu.VMEM(args[1 + k].shape, args[1 + k].dtype) for k in far if k not in into]
    buffers += [pltpu.VMEM(outs[k].shape, outs[k].dtype) for k in far_out if k not in twin]
    count = len(buffers)
    sems = [pltpu.SemaphoreType.DMA((len(v) + 4,)) for v in (far, far_out)]
    return launch(kernel, outs, args, [*buffers, *sems, *scratch], name, where, where_out, us, vmem)


def launch(
    kernel, outs, args, scratch, name, where, where_out, us=0.0, vmem=40, aliases=None
):
    return pl.pallas_call(
        kernel,
        out_shape=[v if w is FREE else w(v.shape, v.dtype) for v, w in zip(outs, where_out)],
        in_specs=[pl.BlockSpec(memory_space=pltpu.SMEM)]
        + [pl.BlockSpec(memory_space=w) for w in where],
        out_specs=[pl.BlockSpec(memory_space=w) for w in where_out],
        scratch_shapes=scratch,
        input_output_aliases=aliases or {},
        compiler_params=pltpu.CompilerParams(vmem_limit_bytes=vmem << 20),
        cost_estimate=pl.CostEstimate(
            flops=int(us * 1e9) + 1000, bytes_accessed=1000, transcendentals=0
        ),
        name=name,
    )(args[0], *[pinned(v, w) for v, w in zip(args[1:], where)])


SPREAD_US, WIDEN_US, FINISH_US, INPUT_US = 0.0, 0.0, 20.0, 10.0


def fwd_kernel(idx_ref, sources, targets, rows_scr, par_scr, u_scr, inner_scr):
    (
        x_in, nw_in, ic_in, icb_in, sc_in, scb_in, tb_in, dl_in, sk_in, gnw_in, seg_in, tp_in,
        ip_in, sp_in, gp_in, op_in, cot_in,
    ) = sources
    (
        normed_ref, gate_ref, inner_ref, pre_ref, mixed_ref, dno_ref, states_ref, spre_ref,
        raw_ref, cols_ref, scols_ref, head_ref, sums_ref, x_part_ref, cot_part_ref, _, _,
    ) = [target.ref for target in targets]
    par_scr[...] = jnp.zeros_like(par_scr)
    nw_ref, x_ref = nw_in(), x_in.ref

    def norm_block(r):
        sl = slice(r * 128, (r + 1) * 128)
        x_in.copies[r].wait()
        v = x_ref[sl, :].astype(F32)
        scale = lax.rsqrt(jnp.mean(v * v, axis=1, keepdims=True) + EPS)
        normed_ref[sl, :] = (v * scale * nw_ref[...].reshape(1, D)).astype(BF)

    for r in range(T // 128):
        norm_block(r)
    x_in.waits = False
    own = pl.ds(pl.multiple_of(idx_ref[0] * GROUP + idx_ref[1] * 64, 64), 64)
    x_part_ref[...] = x_ref[own, :]
    targets[0].put()
    targets[13].put()
    par_scr[0:4, 0:C] = ic_in()[...]
    par_scr[4:5, 0:C] = icb_in()[...].reshape(1, C)
    par_scr[5:6, 0:C] = gnw_in()[...].reshape(1, C)
    par_scr[0:4, C : C + 256] = sc_in()[...]
    par_scr[4:5, C : C + 256] = scb_in()[...].reshape(1, 256)
    par_scr[8:9, 0:NH] = tb_in()[...].reshape(1, NH)
    par_scr[9:10, 0:NH] = dl_in()[...].reshape(1, NH)
    par_scr[10:11, 0:NH] = sk_in()[...].reshape(1, NH)
    par = par_scr[...].T
    cols_ref[...] = par[0:C, 0:8]
    scols_ref[...] = par[C : C + 256, 0:8]
    head_ref[...] = par[0:8, :]
    normed = normed_ref[...]
    raw_ref[0:8, :] = jnp.concatenate(
        [dot_nt(tp_in()[...], normed), jnp.zeros((8 - NH, T), F32)], axis=0
    )
    segf = seg_in()[...].astype(F32)
    raw_ref[8:16, :] = jnp.broadcast_to(segf, (8, T))
    inner_scr[...] = dot_tt(ip_in()[...], normed)
    inner_ref[...] = inner_scr[...].astype(BF).T
    states = dot_tt(sp_in()[...], normed)
    states_ref[...] = states.astype(BF).T
    gate_ref[...] = dot_tt(gp_in()[...], normed)
    for k in (1, 2, 6, 8, 9, 10, 11):
        targets[k].put()
    cot_ref = cot_in()
    dno_ref[...] = dot_nt(op_in()[...], cot_ref[...])
    cot_part_ref[...] = cot_ref[own, :]
    targets[5].put()
    targets[14].put()

    masks = conv_masks(segf)
    head = head_ref[...]
    step = softplus(raw_ref[0:8, :] + head[:, 8:9])
    rate = -jnp.exp(head[:, 9:10])
    logs, lcols = scan_logs(step, rate, rows_scr, segf)

    spre = conv_forward(
        states, [scols_ref[:, k : k + 1] for k in range(KERNEL)], scols_ref[:, 4:5], masks
    )
    spre_ref[...] = spre
    targets[7].put()
    cs = spre * sigmoid(spre)
    b_tok = cs[0:N, :].T.astype(BF)
    c_low = cs[N:, :].astype(BF)
    for h in range(NH):
        hs = slice(h * HD, (h + 1) * HD)
        pre = conv_forward(
            inner_scr[hs, :], [cols_ref[hs, k : k + 1] for k in range(KERNEL)],
            cols_ref[hs, 4:5], masks,
        )
        pre_ref[hs, :] = pre
        u_scr[hs, :] = pre * sigmoid(pre)
    targets[3].put()
    tail, entry = state_rows(logs, segf)
    weighted = u_scr[:, 0:GROUP] * per_head(step[:, 0:GROUP] * tail, GROUP)
    state = dot(weighted.astype(BF), b_tok[0:GROUP, :])
    entering = dot(state.astype(BF), c_low[:, GROUP:])
    for c in range(2):
        sl = slice(c * GROUP, (c + 1) * GROUP)
        neg = link_mask(lcols, segf, c)
        scores = dot(b_tok[sl, :], c_low[:, sl])
        for h in range(NH):
            hs = slice(h * HD, (h + 1) * HD)
            decay = jnp.exp((logs[h : h + 1, sl] - lcols[sl, h : h + 1]) + neg)
            m = (scores * decay).astype(BF)
            u = u_scr[hs, sl]
            y = dot((u * step[h : h + 1, sl]).astype(BF), m)
            if c == 1:
                y = y + entering[hs, :] * entry[h : h + 1, :]
            mixed_ref[hs, sl] = y + head[h : h + 1, 10:11] * u
    targets[4].put()
    squares = jnp.zeros((1, T), F32)
    dots = jnp.zeros((1, T), F32)
    for h in range(NH):
        hs = slice(h * HD, (h + 1) * HD)
        g = gate_ref[hs, :]
        gated = mixed_ref[hs, :] * (g * sigmoid(g))
        squares = squares + jnp.sum(gated * gated, axis=0, keepdims=True)
        dots = dots + jnp.sum(dno_ref[hs, :] * cols_ref[hs, 5:6] * gated, axis=0, keepdims=True)
    sums_ref[...] = jnp.broadcast_to(
        jnp.concatenate([squares, dots], axis=0)[None], sums_ref.shape
    )


def forward(*args):
    outs = [
        sds((T, D), BF), sds((C, T), F32), sds((T, C), BF), sds((C, T), F32), sds((C, T), F32),
        sds((C, T), F32), sds((T, 256), BF), sds((256, T), F32), sds((16, T), F32),
        sds((C, 8), F32), sds((256, 8), F32), sds((8, 128), F32), sds((8, 2, T), F32),
        sds((64, D), BF), sds((64, D), BF), sds((T, D), BF), sds((T, D), BF),
    ]
    scratch = [
        pltpu.VMEM((128, T), F32), pltpu.VMEM((128, 640), F32), pltpu.VMEM((C, T), F32),
        pltpu.VMEM((C, T), F32),
    ]
    return call(
        fwd_kernel, outs, args, scratch, "forward", near_out=(1, 4, 5, 15, 16), into={16: 16},
        twin={0: 15}, split=0,
    )


def mid_kernel(idx_ref, sources, targets, no_scr, low_scr, out_scr, gate_scr, sems):
    sums_in, gate_in, mixed_in, dno_in, cols_in, cot_in, normed_in = sources
    _, no_ref, gate_low_ref, dy_ref, gain_ref = [t.ref for t in targets]
    grads = targets[0]
    total = jnp.sum(sums_in()[...], axis=0)
    scale = lax.rsqrt(total[0:1, :] / INNER + EPS)
    slope = scale * scale * scale * (total[1:2, :] / INNER)
    gate_ref, mixed_ref, dno_ref, cols_ref = gate_in(), mixed_in(), dno_in(), cols_in()
    for h in range(NH):
        hs = slice(h * HD, (h + 1) * HD)
        g = gate_ref[hs, :]
        s = sigmoid(g)
        silu = g * s
        mixed = mixed_ref[hs, :]
        gated = mixed * silu
        gain = cols_ref[hs, 5:6]
        normal = gated * scale
        no_scr[hs, :] = (normal * gain).astype(BF)
        dno = dno_ref[hs, :]
        gain_ref[hs, :] = jnp.broadcast_to(jnp.sum(dno * normal, axis=1, keepdims=True), (HD, 8))
        d_gated = scale * (dno * gain) - gated * slope
        low_scr[hs, :] = (d_gated * mixed * (s * (1.0 + g * (1.0 - s)))).astype(BF)
        dy_ref[hs, :] = (d_gated * silu).astype(BF)
    targets[3].put()
    out_scr[...] = dot(no_scr[...], cot_in()[...]).astype(BF).reshape(4, 96, D)
    for k in range(4):
        source = out_scr.at[:, :, k * C : (k + 1) * C]
        grads.copies.append(
            pltpu.make_async_copy(source, grads.hbm.at[4 * k : 4 * k + 4, 96:192], sems.at[k])
        )
        grads.copies[-1].start()
    no_ref[...] = no_scr[...].T
    gate_low_ref[...] = low_scr[...].T
    targets[1].put()
    targets[2].put()
    gate_scr[...] = dot(low_scr[...], normed_in()[...]).T.astype(BF).reshape(16, 96, C)
    grads.copies.append(pltpu.make_async_copy(gate_scr, grads.hbm.at[:, 0:96], sems.at[4]))
    grads.copies[-1].start()


def middle(*args):
    outs = [
        sds((16, 192, C), BF), sds((T, C), BF), sds((T, C), BF), sds((C, T), BF), sds((C, 8), F32),
    ]
    scratch = [
        pltpu.VMEM((C, T), BF), pltpu.VMEM((C, T), BF), pltpu.VMEM((4, 96, D), BF),
        pltpu.VMEM((16, 96, C), BF), pltpu.SemaphoreType.DMA((5,)),
    ]
    return call(mid_kernel, outs, args, scratch, "middle", near=(1, 2, 3, 5, 6), free=(0,))


def bwd_kernel(
    idx_ref, sources, targets, rows_scr, u_scr, di_scr, mark_scr, cs_scr, dp_scr, tpad, dps_scr,
    grad_scr, tok_scr, low_tok, step_tok, give_scr, inner_scr,
):
    (
        raw_in, head_in, spre_in, pre_in, dy_in, ic_in, inner_in, normed_in, sc_in,
        states_in, gate_low_in, sp_in, tp_in, gp_in, ip_in, no_in, op_in,
    ) = sources
    _, keep_ref, keep_state_ref, extra_ref, give_state_ref, *gives = [
        t.ref for t in targets
    ]
    core = idx_ref[0]
    raw_ref, head_ref, spre_ref = raw_in(), head_in(), spre_in()
    segf = raw_ref[8:9, :]
    later = [
        ((pltpu.roll(segf, T - k, 1) == segf) & (lane_ids(1, T) < T - k)).astype(F32)
        for k in range(1, KERNEL)
    ]
    head = head_ref[...]
    raw = raw_ref[0:8, :] + head[:, 8:9]
    step = softplus(raw)
    rate = -jnp.exp(head[:, 9:10])
    logs, lcols = scan_logs(step, rate, rows_scr, segf, later)
    marks = [jnp.broadcast_to(lcols[:, 9 + k : 10 + k], (T, 128)) for k in range(3)]
    for k in range(3):
        mark_scr[k] = marks[k]
    spre = spre_ref[...]
    cs = spre * sigmoid(spre)
    b_low = cs[0:N, :].astype(BF)
    c_low = cs[N:, :].astype(BF)
    b_tok = cs[0:N, :].T.astype(BF)
    c_tok = cs[N:, :].T.astype(BF)
    pre_ref, dy_ref = pre_in(), dy_in()
    for h in range(NH):
        hs = slice(h * HD, (h + 1) * HD)
        pre = pre_ref[hs, :]
        u_scr[hs, :] = pre * sigmoid(pre)
    tail, entry = state_rows(logs, segf)
    first, second = slice(0, GROUP), slice(GROUP, T)
    weighted = (u_scr[:, first] * per_head(step[:, first] * tail, GROUP)).astype(BF)
    state = dot(weighted, b_tok[first, :]).astype(BF)
    d_entering = (dy_ref[:, second] * per_head(entry, GROUP)).astype(BF)
    d_state = dot(d_entering, c_tok[second, :]).astype(BF)
    entering = dot(state, c_low[:, second])
    into = dot(d_state, b_low[:, first])
    d_c_second = dot_tn(state, d_entering)
    d_b_first = dot_tn(d_state, weighted)
    tri = (row_ids(GROUP, GROUP) >= lane_ids(GROUP, GROUP)).astype(BF)
    before = (row_ids(GROUP, GROUP) < lane_ids(GROUP, GROUP)).astype(F32)
    upto = (row_ids(GROUP, GROUP) < lane_ids(GROUP, GROUP)).astype(F32)
    since = (row_ids(GROUP, GROUP) >= lane_ids(GROUP, GROUP)).astype(F32)
    out_step = []
    out_skip = []
    da_rows = [[None, None] for _ in range(NH)]
    for c in range(2):
        sl = slice(c * GROUP, (c + 1) * GROUP)
        neg = link_mask(lcols, segf, c)
        scores = dot(b_tok[sl, :], c_low[:, sl])
        d_scores = jnp.zeros((GROUP, GROUP), F32)
        for h in range(NH):
            hs = slice(h * HD, (h + 1) * HD)
            decay = jnp.exp((logs[h : h + 1, sl] - lcols[sl, h : h + 1]) + neg)
            m = scores * decay
            dy = dy_ref[hs, sl]
            inflow = (u_scr[hs, sl] * step[h : h + 1, sl]).astype(BF)
            g = dot_tn(inflow, dy)
            d_scores = d_scores + g * decay
            w = dot((g * m).astype(BF), tri)
            da = jnp.sum(w * before, axis=0, keepdims=True)
            da_rows[h][c] = da
            di = dot_nt(dy, m.astype(BF))
            if c == 0:
                di = di + into[hs, :] * tail[h : h + 1, :]
            di_scr[hs, sl] = di
        ds = d_scores.astype(BF)
        d_b = dot_nt(c_low[:, sl], ds)
        d_c = dot(b_low[:, sl], ds)
        if c == 0:
            d_b = d_b + d_b_first
        else:
            d_c = d_c + d_c_second
        cs_scr[0:N, sl] = d_b
        cs_scr[N:, sl] = d_c
    ic_ref, inner_ref, normed_ref = ic_in(), inner_in(), normed_in()
    zero = jnp.zeros((1, GROUP), F32)
    q_rows, e_rows = [], []
    for h in range(NH):
        hs = slice(h * HD, (h + 1) * HD)
        q = u_scr[hs, first] * step[h : h + 1, first] * into[hs, :]
        q_rows.append(jnp.sum(q, axis=0, keepdims=True))
        e = dy_ref[hs, second] * entering[hs, :]
        e_rows.append(jnp.sum(e, axis=0, keepdims=True))
    q8 = jnp.concatenate(q_rows + [zero, zero], axis=0) * tail
    e8 = jnp.concatenate(e_rows + [zero, zero], axis=0) * entry
    da0 = jnp.concatenate([da_rows[h][0] for h in range(NH)] + [zero, zero], axis=0)
    da1 = jnp.concatenate([da_rows[h][1] for h in range(NH)] + [zero, zero], axis=0)
    da = jnp.concatenate([da0 + dot(q8, upto, EXACT), da1 + dot(e8, since, EXACT)], axis=1)
    d_steps = []
    for h in range(NH):
        hs = slice(h * HD, (h + 1) * HD)
        pre = pre_ref[hs, :]
        s = sigmoid(pre)
        u = u_scr[hs, :]
        di = di_scr[hs, :]
        dy = dy_ref[hs, :].astype(F32)
        d_steps.append(jnp.sum(di * u, axis=0, keepdims=True))
        out_skip.append(jnp.sum(dy * u, axis=0, keepdims=True))
        d_u = di * step[h : h + 1, :] + head[h : h + 1, 10:11] * dy
        d_pre = d_u * (s * (1.0 + pre * (1.0 - s)))
        di_scr[hs, :] = d_pre
    zero = jnp.zeros((2, T), F32)
    d_step = jnp.concatenate(d_steps + [zero], axis=0) + da * rate
    skips = jnp.concatenate(out_skip + [zero], axis=0)
    d_raw = d_step * sigmoid(raw)
    dp_scr[0:T, :] = di_scr[...].T
    dp_scr[T:, :] = jnp.zeros((8, C), F32)
    rows = conv_backward(dp_scr, inner_ref, ic_ref, mark_scr, low_tok)
    inner_grad = dot_tn(normed_ref[...], low_tok[...]).astype(BF)
    inner_scr[...] = inner_grad.reshape(16, 96, C)
    buffer = targets[0]
    buffer.copies.append(pltpu.make_async_copy(inner_scr, buffer.hbm.at[:, 0:96], buffer.sem))
    buffer.copies[-1].start()
    rows_scr[...] = jnp.zeros_like(rows_scr)
    rows_scr[0:8, :] = d_raw
    step_tok[...] = rows_scr[...].T.astype(BF)
    extra_ref[0:8, :] = dot(d_raw.astype(BF), normed_ref[...])
    sc_ref, states_ref = sc_in(), states_in()
    for part in range(4):
        rs = slice(part * 64, (part + 1) * 64)
        pre = spre_ref[rs, :]
        s = sigmoid(pre)
        cs_scr[rs, :] = cs_scr[rs, :] * (s * (1.0 + pre * (1.0 - s)))
    dps_scr[0:T, :] = cs_scr[...].T
    dps_scr[T:, :] = jnp.zeros((8, 256), F32)
    state_rows_ = conv_backward(dps_scr, states_ref, sc_ref, mark_scr, tok_scr)
    columns = [
        jnp.sum(d_raw, axis=1, keepdims=True), jnp.sum(da * step, axis=1, keepdims=True) * rate,
        jnp.sum(skips, axis=1, keepdims=True), jnp.zeros((8, 125), F32),
    ]
    extra_ref[8:16, :] = jnp.concatenate(
        [rows, *columns, jnp.zeros((8, D - C - 128), F32)], axis=1
    )
    targets[3].put()
    taps = jnp.concatenate(
        [
            jnp.concatenate([state_rows_, jnp.zeros((8, D - 256), F32)], axis=1),
            jnp.zeros((8, D), F32),
        ],
        axis=0,
    ).astype(BF)
    grad_scr[...] = dot_tn(tok_scr[...], normed_ref[...]).astype(BF)
    tpad[...] = jnp.zeros_like(tpad)
    tpad[0:NH, :] = tp_in()[...]
    gate_low_ref, no_ref = gate_low_in(), no_in()
    gp_ref, ip_ref, sp_ref, op_ref = gp_in(), ip_in(), sp_in(), op_in()
    for give, half in ((True, 1 - core), (False, core)):
        tok = pl.ds(pl.multiple_of(half * GROUP, GROUP), GROUP)
        total = dot_nt(gate_low_ref[tok, :], gp_ref[...])
        total = total + dot_nt(low_tok[tok, :], ip_ref[...])
        total = total + dot_nt(tok_scr[tok, :], sp_ref[...])
        total = (total + dot(step_tok[tok, :], tpad[...])).astype(BF)
        out = dot(no_ref[tok, :], op_ref[...]).astype(BF)
        for k in range(4):
            slot = lax.rem(k + 4 - idx_ref[1], 4)
            rows = pl.ds(pl.multiple_of(half * 128 + k * 32, 32), 32)
            ref, state_ref = (give_scr, give_state_ref) if give else (keep_ref, keep_state_ref)
            ref[slot, 0:64, :] = total[k * 64 : (k + 1) * 64, :]
            ref[slot, 64:128, :] = out[k * 64 : (k + 1) * 64, :]
            state_ref[slot, 0:32, :] = grad_scr[rows, :]
            state_ref[slot, 32:48, :] = taps
        if give:
            for k in range(4):
                gives[k][...] = give_scr[k]


def backward(*args):
    outs = [
        sds((16, 112, C), BF), sds((4, 128, D), BF), sds((4, 48, D), BF), sds((16, D), F32),
        sds((4, 48, D), BF), *[sds((128, D), BF)] * 4,
    ]
    scratch = [
        pltpu.VMEM((128, T), F32), pltpu.VMEM((C, T), F32), pltpu.VMEM((C, T), F32),
        pltpu.VMEM((3, T, 128), F32), pltpu.VMEM((256, T), F32), pltpu.VMEM((T + 8, C), F32),
        pltpu.VMEM((128, D), BF), pltpu.VMEM((T + 8, 256), F32), pltpu.VMEM((256, D), BF),
        pltpu.VMEM((T, 256), BF), pltpu.VMEM((T, C), BF), pltpu.VMEM((T, 128), BF),
        pltpu.VMEM((4, 128, D), BF), pltpu.VMEM((16, 96, C), BF),
    ]
    return call(
        bwd_kernel, outs, args, scratch, "backward",
        near_out=(1, 2, 4, 5, 6, 7, 8),
    )


def fold_kernel(idx_ref, *refs):
    keep, keep_state, got_state, *got = refs[:7]
    own_hbm, own_state_hbm, *sends = refs[7:15]
    own, own_state, sems = refs[15:]
    stores = [
        pltpu.make_async_copy(own_state, own_state_hbm, sems.at[0]),
        pltpu.make_async_copy(own, own_hbm, sems.at[1]),
    ]
    own[...] = keep[0].astype(F32) + got[0][...].astype(F32)
    stores[1].start()
    own_state[...] = keep_state[0].astype(F32) + got_state[0].astype(F32)
    stores[0].start()
    for k in range(1, 4):
        sends[k - 1][...] = (keep_state[k].astype(F32) + got_state[k].astype(F32)).astype(BF)
        sends[k + 2][...] = (keep[k].astype(F32) + got[k][...].astype(F32)).astype(BF)
    for store in stores:
        store.wait()


def swap(v):
    return lax.ppermute(v, "core", [(0, 1), (1, 0)])


def turn(v, axis, by):
    return lax.ppermute(v, axis, [(i, (i + by) % 4) for i in range(4)])


def scatter(idx, keep, keep_state, give_state, gives):
    rows, state_rows = sds((128, D), BF), sds((48, D), BF)
    outs = [sds((128, D), F32), sds((48, D), F32), *[state_rows] * 3, *[rows] * 3]
    scratch = [
        pltpu.VMEM((128, D), F32), pltpu.VMEM((48, D), F32), pltpu.SemaphoreType.DMA((2,)),
    ]
    own, own_state, *sends = launch(
        fold_kernel, outs, (idx, keep, keep_state, swap(give_state), *map(swap, gives)), scratch,
        "fold", [NEAR] * 7, [FAR] * 2 + [NEAR] * 6, vmem=16,
    )
    sends = [turn(send, "y", k % 3 + 1) for k, send in enumerate(sends)]
    return [own_state, *sends[:3]], [own, *sends[3:]]


def spread_out(chunk):
    return [chunk] + [turn(chunk, "y", k) for k in range(1, 4)]


def gather(pieces, *earlier):
    return pieces + [swap(after(piece, *earlier)) for piece in pieces]


def place_of(idx_ref, k):
    half = idx_ref[0] if k < 4 else 1 - idx_ref[0]
    return half, half * 4 + lax.rem(idx_ref[1] + 4 - k % 4, 4)


def finish_kernel(idx_ref, *refs):
    pieces, out_hbm, grad_hbm = refs[:8], refs[8], refs[9]
    buf, grad, in_sems, out_sems = refs[10:]
    loads = [pltpu.make_async_copy(pieces[k], buf.at[k], in_sems.at[k]) for k in range(8)]
    for load in loads:
        load.start()
    stores = []
    for k in range(8):
        _, place = place_of(idx_ref, k)
        rows = pl.ds(pl.multiple_of(place * 64, 64), 64)
        loads[k].wait()
        stores.append(
            pltpu.make_async_copy(buf.at[k, 64:128], out_hbm.at[rows], out_sems.at[0, k])
        )
        stores[-1].start()
        grad[k] = buf[k, 0:64, :].astype(F32)
        stores.append(pltpu.make_async_copy(grad.at[k], grad_hbm.at[rows], out_sems.at[1, k]))
        stores[-1].start()
    for store in stores:
        store.wait()


def ends_kernel(idx_ref, sources, targets, state_scr, small_scr):
    (
        state_ref, norm_ref, sconv_ref, sbias_ref, step_ref, taps_ref, bias_ref, tb_ref, dl_ref,
        sk_ref, gnw_ref,
    ) = [t.ref for t in targets]
    for k in range(8):
        _, place = place_of(idx_ref, k)
        piece = sources[k]()
        for j in range(4):
            columns = slice(j * C, (j + 1) * C)
            for half in range(2):
                rows = pl.ds(pl.multiple_of(place * 32 + half * 16, 16), 16)
                state_scr[rows, columns] = piece[j * 4 + half].astype(F32)
            small_scr[place, :, columns] = piece[j * 4 + 2].astype(F32)
    for row in range(12):
        sl = slice(row * 128, (row + 1) * 128)
        state_ref[sl, :] = state_scr[:, sl].T
    targets[0].put()
    sconv_ref[...] = small_scr[0, 0:4, 0:256]
    sbias_ref[...] = small_scr[0, 4:5, 0:256].reshape(256)
    norm = small_scr[0, 8:9, :]
    for k in range(1, 8):
        norm = norm + small_scr[k, 8:9, :]
    norm_ref[...] = norm.reshape(D)
    own = sources[0]()
    for j in range(4):
        step_ref[:, j * C : (j + 1) * C] = own[j * 4 + 3][0:NH, :].astype(F32)
    smalls = jnp.concatenate([own[3], own[7]], axis=1)[8:16, :].astype(F32)
    taps_ref[...] = smalls[0:4, 0:C]
    bias_ref[...] = smalls[4:5, 0:C].reshape(C)
    gnw_ref[...] = smalls[5:6, 0:C].reshape(C)
    heads = jnp.concatenate([smalls[:, C : C + 128], jnp.zeros((120, 128), F32)], axis=0).T
    tb_ref[...] = heads[0:1, 0:NH].reshape(NH)
    dl_ref[...] = heads[1:2, 0:NH].reshape(NH)
    sk_ref[...] = heads[2:3, 0:NH].reshape(NH)


def pack_kernel(idx_ref, *refs):
    buf_hbm, own_any, p1_any, p2_any, p3_any, extra_hbm, gain_hbm, out_hbm = refs[:8]
    own, parts, extra, gain, pad, blocks, sems = refs[8:]
    loads = [
        pltpu.make_async_copy(source, target, sems.at[k])
        for k, (source, target) in enumerate(
            (
                (own_any, own), (p1_any, parts.at[0]), (p2_any, parts.at[1]),
                (p3_any, parts.at[2]), (extra_hbm, extra), (gain_hbm, gain),
            )
        )
    ]
    for load in loads:
        load.start()
    for load in loads:
        load.wait()
    total = (own[...] + parts[0].astype(F32)) + (parts[1].astype(F32) + parts[2].astype(F32))
    pad[...] = jnp.zeros_like(pad)
    pad[:, 5:6] = gain[:, 0:1]
    gain_row = jnp.concatenate([pad[...].T[0:8, :], jnp.zeros((8, D - C), F32)], axis=1)
    rows = [
        total[0:16, :], total[16:32, :],
        jnp.concatenate([total[32:40, :], jnp.zeros((8, D), F32)], axis=0),
        jnp.concatenate([extra[0:8, :], extra[8:16, :] + gain_row], axis=0),
    ]
    for k in range(16):
        blocks[k] = rows[k % 4][:, k // 4 * C : (k // 4 + 1) * C].astype(BF)
    store = pltpu.make_async_copy(blocks, out_hbm.at[:, 96:112], sems.at[6])
    store.start()
    store.wait()


def input_kernel(idx_ref, sources, targets):
    x_ref, cot_ref, nw_ref = [source() for source in sources[:3]]
    chunk_ref, norm_ref = [t.ref for t in targets]
    p0, p1, p2, p3 = [source() for source in sources[3:]]
    total = (p0[...] + p1[...].astype(F32)) + (p2[...].astype(F32) + p3[...].astype(F32))
    d_normed = total[0:64, :]
    v = x_ref[...].astype(F32)
    scale = lax.rsqrt(jnp.mean(v * v, axis=1, keepdims=True) + EPS)
    weighted = d_normed * nw_ref[...].reshape(1, D)
    grad = scale * weighted - v * (
        scale * scale * scale * jnp.mean(weighted * v, axis=1, keepdims=True)
    )
    chunk_ref[0:64, :] = (cot_ref[...].astype(F32) + grad).astype(BF)
    chunk_ref[64:128, :] = (v + total[64:128, :]).astype(BF)
    targets[0].put()
    norm = jnp.sum(d_normed * v * scale, axis=0, keepdims=True)
    rows = [norm[:, k * C : (k + 1) * C] for k in range(4)]
    norm_ref[...] = jnp.concatenate([*rows, jnp.zeros((12, C), F32)], axis=0).astype(BF)


def share_kernel(idx_ref, sources, targets):
    parts_ref, out_ref = sources[0](), targets[0].ref
    norm = parts_ref[0, 16:32, :].astype(F32)
    for k in range(1, 16):
        norm = norm + parts_ref[k, 16:32, :].astype(F32)
    for k in range(16):
        if k % 4 == 2:
            row = jnp.concatenate(
                [jnp.zeros((8, C), F32), norm[k // 4 : k // 4 + 1, :], jnp.zeros((7, C), F32)],
                axis=0,
            )
            out_ref[k] = (parts_ref[k, 0:16, :].astype(F32) + row).astype(BF)
        else:
            out_ref[k] = parts_ref[k, 0:16, :]


def total_of(parts_ref):
    total = parts_ref[0].astype(F32)
    for k in range(1, 16):
        total = total + parts_ref[k].astype(F32)
    return total.astype(BF)


def reduce_kernel(idx_ref, sources, targets):
    targets[0].ref[...] = total_of(sources[0]())


def spread_kernel(
    idx_ref, terms_any, first_any, norm_any, small_hbm, wide_hbm, terms, first, norm, own, small,
    load_sems, sems,
):
    pairs = [(terms_any.at[4 * k : 4 * k + 4], terms.at[4 * k : 4 * k + 4]) for k in range(4)]
    pairs += [(first_any, first), (norm_any, norm)]
    loads = [
        pltpu.make_async_copy(source, target, load_sems.at[k])
        for k, (source, target) in enumerate(pairs)
    ]
    for load in loads:
        load.start()
    total = jnp.zeros((112, C), F32)
    for k in range(4):
        loads[k].wait()
        part = terms[4 * k].astype(F32)
        for j in range(1, 4):
            part = part + terms[4 * k + j].astype(F32)
        total = total + part
    own[...] = total.astype(BF)
    loads[4].wait()
    stores = [
        pltpu.make_async_copy(own.at[0:96], wide_hbm.at[k, 192:288], sems.at[k])
        for k in range(4)
    ]
    stores += [
        pltpu.make_async_copy(first, wide_hbm.at[k, 0:192], sems.at[4 + k]) for k in range(4)
    ]
    for store in stores:
        store.start()
    loads[5].wait()
    both = jnp.concatenate([own[96:112, :], norm[...]], axis=0)
    for k in range(16):
        small[k] = both
    stores.append(pltpu.make_async_copy(small, small_hbm, sems.at[8]))
    stores[-1].start()
    for store in stores:
        store.wait()


def again_kernel(idx_ref, blocks_any, out_hbm, blocks, load_sem, sems):
    load = pltpu.make_async_copy(blocks_any, blocks, load_sem)
    load.start()
    load.wait()
    stores = [pltpu.make_async_copy(blocks, out_hbm.at[k], sems.at[k]) for k in range(4)]
    for store in stores:
        store.start()
    for store in stores:
        store.wait()


def widen_kernel(
    idx_ref, hbm, gate_hbm, out_hbm, inner_hbm, buf, gate, out, inner, in_sems, out_sems
):
    loads = [pltpu.make_async_copy(hbm.at[k], buf.at[k], in_sems.at[k]) for k in range(4)]
    for load in loads:
        load.start()
    stores = []
    for k in range(4):
        loads[k].wait()
        for j in range(4):
            gate[k, j] = buf[k, j, 0:96, :].astype(F32)
            out[k, j * 96 : (j + 1) * 96, :] = buf[k, j, 96:192, :].astype(F32)
            inner[k, j] = buf[k, j, 192:288, :].astype(F32)
        columns = slice(k * C, (k + 1) * C)
        for j, (source, target) in enumerate(
            (
                (gate.at[k], gate_hbm.at[k]), (out.at[k], out_hbm.at[:, columns]),
                (inner.at[k], inner_hbm.at[k]),
            )
        ):
            stores.append(pltpu.make_async_copy(source, target, out_sems.at[j, k]))
            stores[-1].start()
    for store in stores:
        store.wait()


def flat(z, x, y, core):
    return ((z * 4 + x) * 4 + y) * 2 + core


def teams(kind):
    out = []
    for core in range(2):
        for y in range(4):
            grid = [
                [flat(b, a, y, 0) if core == 0 else flat(a, b, y, 1) for b in range(4)]
                for a in range(4)
            ]
            if kind == "both":
                out.append([place for row in grid for place in row])
            elif kind == "second":
                out.extend(grid)
            else:
                out.extend([list(column) for column in zip(*grid)])
    return out


def exchange(v, kind):
    return lax.all_to_all(
        v, ("z", "x", "y", "core"), 0, 0, axis_index_groups=teams(kind), tiled=True
    )


def after(idx, *values):
    return lax.optimization_barrier((idx, *values))[0]


def per_device(
    inputs, norm_weight, gate_proj, inner_proj, state_proj, step_proj, inner_conv,
    inner_conv_bias, state_conv, state_conv_bias, step_bias, decay_log, skip_weight,
    gated_norm_weight, out_proj, segments, cotangent,
):
    x, cot, step_rows = inputs[0], cotangent[0], step_proj.T
    dma = pltpu.SemaphoreType.DMA
    idx = jnp.stack([lax.axis_index(a) for a in ("core", "y", "x", "z")]).astype(jnp.int32)
    (
        normed, gate, inner, pre, mixed, dno, states, spre, raw, cols, scols, head, sums, x_part,
        cot_part, normed_here, cot_here,
    ) = forward(
        idx, x, norm_weight, inner_conv, inner_conv_bias, state_conv, state_conv_bias, step_bias,
        decay_log, skip_weight, gated_norm_weight, segments, step_rows, inner_proj, state_proj,
        gate_proj, out_proj, cot,
    )
    sums = lax.all_to_all(sums, ("y", "core"), 0, 0, tiled=True)
    grads, no, gate_low, dy, gain = middle(
        idx, sums, gate, mixed, dno, cols, cot_here, normed_here
    )

    first_terms = exchange(grads, "both")
    inner_grad, keep, keep_state, extra, give_state, *gives = backward(
        idx, raw, head, spre, pre, dy, inner_conv, inner, normed, state_conv, states, gate_low, state_proj,
        step_rows, gate_proj, inner_proj, no, out_proj,
    )
    state_pieces, pieces = scatter(idx, keep, keep_state, give_state, gives)
    (terms,) = launch(
        pack_kernel, [sds((16, 112, C), BF)], (idx, inner_grad, *state_pieces, extra, gain),
        [
            pltpu.VMEM((48, D), F32), pltpu.VMEM((3, 48, D), BF), pltpu.VMEM((16, D), F32),
            pltpu.VMEM((C, 8), F32), pltpu.VMEM((C, 128), F32), pltpu.VMEM((16, 16, C), BF),
            dma((7,)),
        ],
        "pack", [FAR, FAR, FREE, FREE, FREE, FAR, FAR], [FAR], aliases={1: 0},
    )
    second_terms = exchange(terms, "both")
    (first,) = call(
        reduce_kernel, [sds((192, C), BF)], (idx, first_terms), name="reduce", free=(0,),
    )
    chunk, norm = call(
        input_kernel, [sds((128, D), BF), sds((16, C), BF)],
        (idx, x_part, cot_part, norm_weight, *pieces), (), "input_part", free=(4, 5, 6),
        free_out=(0,), us=INPUT_US,
    )
    small, wide = launch(
        spread_kernel, [sds((16, 32, C), BF), sds((4, 288, C), BF)],
        (idx, second_terms, first, norm),
        [
            pltpu.VMEM((16, 112, C), BF), pltpu.VMEM((192, C), BF), pltpu.VMEM((16, C), BF),
            pltpu.VMEM((112, C), BF), pltpu.VMEM((16, 32, C), BF), dma((6,)), dma((9,)),
        ],
        "spread", [FREE, FAR, FAR], [FAR] * 2, SPREAD_US,
    )
    small = exchange(small, "both")
    chunks = spread_out(chunk)
    wide = exchange(after(wide, small, *chunks[1:]), "second")
    (pack,) = call(
        share_kernel, [sds((16, 16, C), BF)], (idx, small), name="share", free=(0,),
        free_out=(0,),
    )
    (wide,) = launch(
        again_kernel, [sds((4, 4, 288, C), BF)], (idx, wide),
        [pltpu.VMEM((4, 288, C), BF), dma(()), dma((4,))], "again", [FREE], [FAR],
    )
    parts = gather(chunks, wide)
    ends = gather(spread_out(pack), wide)
    outputs, input_grad = launch(
        finish_kernel, [sds((T, D), BF), sds((T, D), F32)], (idx, *parts),
        [
            pltpu.VMEM((8, 128, D), BF), pltpu.VMEM((8, 64, D), F32), dma((8,)), dma((2, 8)),
        ],
        "finish", [FREE] * 8, [FAR] * 2, FINISH_US,
    )
    wide = exchange(wide, "first")
    (
        state_grad, norm_grad, sconv, sbias, step_grad, taps, bias, tb, dl, sk, gnw,
    ) = call(
        ends_kernel,
        [
            sds((D, 256), F32), sds((D,), F32), sds((KERNEL, 256), F32), sds((256,), F32),
            sds((NH, D), F32), sds((KERNEL, C), F32), sds((C,), F32), sds((NH,), F32),
            sds((NH,), F32), sds((NH,), F32), sds((C,), F32),
        ],
        (idx, *ends), [pltpu.VMEM((256, D), F32), pltpu.VMEM((8, 16, D), F32)], "ends",
        free=range(8),
    )
    gate_grad, out_grad, inner_grad = launch(
        widen_kernel,
        [sds((4, 4, 96, C), F32), sds((C, D), F32), sds((4, 4, 96, C), F32)], (idx, wide),
        [
            pltpu.VMEM((4, 4, 288, C), BF), pltpu.VMEM((4, 4, 96, C), F32),
            pltpu.VMEM((4, C, C), F32), pltpu.VMEM((4, 4, 96, C), F32), dma((4,)), dma((3, 4)),
        ],
        "widen", [FREE], [FAR] * 3, WIDEN_US,
    )
    return (
        outputs[None], input_grad[None], norm_grad, gate_grad.reshape(D, C),
        inner_grad.reshape(D, C), state_grad, step_grad.T, taps, bias, sconv, sbias, tb, dl, sk,
        gnw, out_grad,
    )


def solution(mesh):
    small = Mesh(mesh.devices.reshape(4, 4, 4, 2), ("z", "x", "y", "core"))
    dp, tp = ("z", "x"), ("y", "core")
    placed = (
        P(dp, None, None), P(), P(None, tp), P(None, tp), P(), P(None, tp), P(None, tp), P(tp),
        P(), P(), P(tp), P(tp), P(tp), P(tp), P(tp, None), P(dp, None), P(dp, None, None),
    )
    out = (
        P(dp, None, None), P(dp, None, None), P(), P(None, tp), P(None, tp), P(), P(None, tp),
        P(None, tp), P(tp), P(), P(), P(tp), P(tp), P(tp), P(tp), P(tp, None),
    )
    return jax.shard_map(per_device, mesh=small, in_specs=placed, out_specs=out, check_vma=False)
```

```python
import functools

import jax
import jax.numpy as jnp
from jax import lax
from jax.experimental import pallas as pl
from jax.experimental.pallas import tpu as pltpu
from jax.sharding import Mesh, PartitionSpec as P

KERNEL = 4
INNER = 3072
EPS = 1e-05
T = 512
GROUP = 256
D = 1536
C = 384
NH = 6
HD = 64
N = 128
BF = jnp.bfloat16
F32 = jnp.float32
EXACT = lax.Precision.HIGHEST


def dot(a, b, precision=None):
    return jnp.dot(a, b, preferred_element_type=F32, precision=precision)


def dot_nt(a, b):
    return lax.dot_general(a, b, (((1,), (1,)), ((), ())), preferred_element_type=F32)


def dot_tt(a, b):
    return lax.dot_general(a, b, (((0,), (1,)), ((), ())), preferred_element_type=F32)


def dot_tn(a, b):
    return lax.dot_general(a, b, (((0,), (0,)), ((), ())), preferred_element_type=F32)


def sigmoid(v):
    return 1.0 / (1.0 + jnp.exp(-v))


def softplus(v):
    return jnp.maximum(v, 0.0) + jnp.log1p(jnp.exp(-jnp.abs(v)))


def lane_ids(rows, cols):
    return lax.broadcasted_iota(jnp.int32, (rows, cols), 1)


def row_ids(rows, cols):
    return lax.broadcasted_iota(jnp.int32, (rows, cols), 0)


def conv_masks(seg):
    lanes = lane_ids(1, T)
    out = []
    for k in range(1, KERNEL):
        same = (pltpu.roll(seg, k, 1) == seg) & (lanes >= k)
        out.append(same.astype(F32))
    return out


def conv_forward(v, cols, bias, masks):
    total = bias + cols[0] * v
    for k in range(1, KERNEL):
        total = total + cols[k] * (pltpu.roll(v, k, 1) * masks[k - 1])
    return total


def conv_backward(dp_scr, v_ref, taps_ref, mark_scr, out_ref):
    width = v_ref.shape[1]
    rows = 32
    taps = [jnp.zeros((8, width), F32) for _ in range(KERNEL + 1)]

    def fold(v):
        return jnp.sum(v.reshape(rows // 8, 8, width), axis=0)

    for first in range(0, T, rows):
        here = slice(first, first + rows)
        v = v_ref[here, :].astype(F32)
        d_pre = dp_scr[here, :]
        total = taps_ref[0:1, :] * d_pre
        taps[0] = taps[0] + fold(d_pre * v)
        taps[KERNEL] = taps[KERNEL] + fold(d_pre)
        for k in range(1, KERNEL):
            mark = jnp.concatenate([mark_scr[k - 1, here, :]] * (width // 128), axis=1)
            back = dp_scr[first + k : first + k + rows, :] * mark
            total = total + taps_ref[k : k + 1, :] * back
            taps[k] = taps[k] + fold(back * v)
        out_ref[here, :] = total.astype(BF)
    sums = [jnp.sum(tap, axis=0, keepdims=True) for tap in taps]
    return jnp.concatenate([*sums, jnp.zeros((3, width), F32)], axis=0)


def scan_logs(step, rate, rows_ref, segf, more=()):
    upper = (row_ids(GROUP, GROUP) <= lane_ids(GROUP, GROUP)).astype(F32)
    a = step * rate
    logs = jnp.concatenate(
        [dot(a[:, :GROUP], upper, EXACT), dot(a[:, GROUP:], upper, EXACT)], axis=1
    )
    rows_ref[...] = jnp.zeros_like(rows_ref)
    rows_ref[0:8, :] = logs
    rows_ref[8:9, :] = segf
    for k, row in enumerate(more):
        rows_ref[9 + k : 10 + k, :] = row
    return logs, rows_ref[...].T


def link_mask(cols, segf, c):
    sl = slice(c * GROUP, (c + 1) * GROUP)
    same = cols[sl, 8:9] == segf[:, sl]
    later = lane_ids(GROUP, GROUP) >= row_ids(GROUP, GROUP)
    return jnp.where(same & later, 0.0, -1e30)


def state_rows(logs, segf):
    final = segf[:, GROUP - 1 : GROUP]
    tail = jnp.exp(logs[:, GROUP - 1 : GROUP] - logs[:, :GROUP]) * (
        segf[:, :GROUP] == final
    ).astype(F32)
    entry = jnp.exp(logs[:, GROUP:]) * (segf[:, GROUP:] == final).astype(F32)
    return tail, entry


def per_head(rows, width):
    return jnp.concatenate(
        [jnp.broadcast_to(rows[h : h + 1, :], (HD, width)) for h in range(NH)], axis=0
    )


class Source:
    def __init__(self, hbm, vmem, sem):
        self.ref, self.waits = vmem, True
        if isinstance(sem, list):
            rows = vmem.shape[0] // len(sem)
            parts = [slice(k * rows, (k + 1) * rows) for k in range(len(sem))]
            self.copies = [
                pltpu.make_async_copy(hbm.at[part], vmem.at[part], one)
                for part, one in zip(parts, sem)
            ]
        else:
            self.copies = [pltpu.make_async_copy(hbm, vmem, sem)]
        for copy in self.copies:
            copy.start()

    def __call__(self):
        if self.waits:
            for copy in self.copies:
                copy.wait()
            self.waits = False
        return self.ref


class Target:
    def __init__(self, hbm, vmem, sem):
        self.hbm, self.ref, self.sem = hbm, vmem, sem
        self.copies = []

    def put(self):
        self.copies.append(pltpu.make_async_copy(self.ref, self.hbm, self.sem))
        self.copies[-1].start()


def sds(shape, dtype):
    return jax.ShapeDtypeStruct(shape, dtype)


class Here:
    def __init__(self, ref):
        self.ref = ref

    def __call__(self):
        return self.ref

    def put(self):
        pass


NEAR, FAR, FREE = pltpu.VMEM, pltpu.HBM, pl.ANY


def pinned(v, where):
    return v if where is FREE else pltpu.with_memory_space_constraint(v, where)


def call(
    body, outs, args, scratch=(), name=None, near=(), free=(), near_out=(), free_out=(), us=0.0,
    vmem=40, into=None, twin=None, split=None,
):
    into, twin = into or {}, twin or {}
    n, m = len(args) - 1, len(outs)
    where = [NEAR if k in near else FREE if k in free else FAR for k in range(n)]
    where_out = [NEAR if k in near_out else FREE if k in free_out else FAR for k in range(m)]
    far = [k for k in range(n) if k not in near]
    far_out = [k for k in range(m) if k not in near_out]

    def kernel(idx_ref, *refs):
        ins, results, rest = refs[:n], refs[n : n + m], refs[n + m :]
        *buffers, in_sems, out_sems = rest[: count + 2]
        own = rest[count + 2 :]
        sources, targets = [Here(ref) for ref in ins], [Here(ref) for ref in results]
        for j, k in enumerate(far):
            buffer = results[into[k]] if k in into else buffers.pop(0)
            sem = in_sems.at[j]
            if k == split:
                sem = [sem, *[in_sems.at[len(far) + i] for i in range(3)]]
            sources[k] = Source(ins[k], buffer, sem)
        for j, k in enumerate(far_out):
            buffer = results[twin[k]] if k in twin else buffers.pop(0)
            targets[k] = Target(results[k], buffer, out_sems.at[j])
        body(idx_ref, sources, targets, *own)
        for source in sources:
            source()
        for k in far_out:
            if not targets[k].copies:
                targets[k].put()
        for k in far_out:
            for copy in targets[k].copies:
                copy.wait()

    buffers = [pltpu.VMEM(args[1 + k].shape, args[1 + k].dtype) for k in far if k not in into]
    buffers += [pltpu.VMEM(outs[k].shape, outs[k].dtype) for k in far_out if k not in twin]
    count = len(buffers)
    sems = [pltpu.SemaphoreType.DMA((len(v) + 4,)) for v in (far, far_out)]
    return launch(kernel, outs, args, [*buffers, *sems, *scratch], name, where, where_out, us, vmem)


def launch(
    kernel, outs, args, scratch, name, where, where_out, us=0.0, vmem=40, aliases=None
):
    return pl.pallas_call(
        kernel,
        out_shape=[v if w is FREE else w(v.shape, v.dtype) for v, w in zip(outs, where_out)],
        in_specs=[pl.BlockSpec(memory_space=pltpu.SMEM)]
        + [pl.BlockSpec(memory_space=w) for w in where],
        out_specs=[pl.BlockSpec(memory_space=w) for w in where_out],
        scratch_shapes=scratch,
        input_output_aliases=aliases or {},
        compiler_params=pltpu.CompilerParams(vmem_limit_bytes=vmem << 20),
        cost_estimate=pl.CostEstimate(
            flops=int(us * 1e9) + 1000, bytes_accessed=1000, transcendentals=0
        ),
        name=name,
    )(args[0], *[pinned(v, w) for v, w in zip(args[1:], where)])


SPREAD_US, WIDEN_US, FINISH_US, INPUT_US = 0.0, 0.0, 20.0, 10.0


def fwd_kernel(idx_ref, sources, targets, rows_scr, par_scr, u_scr, inner_scr):
    (
        x_in, nw_in, ic_in, icb_in, sc_in, scb_in, tb_in, dl_in, sk_in, gnw_in, seg_in, tp_in,
        ip_in, sp_in, gp_in, op_in, cot_in,
    ) = sources
    (
        normed_ref, gate_ref, inner_ref, pre_ref, mixed_ref, dno_ref, states_ref, spre_ref,
        raw_ref, cols_ref, scols_ref, head_ref, sums_ref, x_part_ref, cot_part_ref, _, _,
    ) = [target.ref for target in targets]
    par_scr[...] = jnp.zeros_like(par_scr)
    nw_ref, x_ref = nw_in(), x_in.ref

    def norm_block(r):
        sl = slice(r * 128, (r + 1) * 128)
        x_in.copies[r].wait()
        v = x_ref[sl, :].astype(F32)
        scale = lax.rsqrt(jnp.mean(v * v, axis=1, keepdims=True) + EPS)
        normed_ref[sl, :] = (v * scale * nw_ref[...].reshape(1, D)).astype(BF)

    for r in range(T // 128):
        norm_block(r)
    x_in.waits = False
    own = pl.ds(pl.multiple_of(idx_ref[0] * GROUP + idx_ref[1] * 64, 64), 64)
    x_part_ref[...] = x_ref[own, :]
    targets[0].put()
    targets[13].put()
    par_scr[0:4, 0:C] = ic_in()[...]
    par_scr[4:5, 0:C] = icb_in()[...].reshape(1, C)
    par_scr[5:6, 0:C] = gnw_in()[...].reshape(1, C)
    par_scr[0:4, C : C + 256] = sc_in()[...]
    par_scr[4:5, C : C + 256] = scb_in()[...].reshape(1, 256)
    par_scr[8:9, 0:NH] = tb_in()[...].reshape(1, NH)
    par_scr[9:10, 0:NH] = dl_in()[...].reshape(1, NH)
    par_scr[10:11, 0:NH] = sk_in()[...].reshape(1, NH)
    par = par_scr[...].T
    cols_ref[...] = par[0:C, 0:8]
    scols_ref[...] = par[C : C + 256, 0:8]
    head_ref[...] = par[0:8, :]
    normed = normed_ref[...]
    raw_ref[0:8, :] = jnp.concatenate(
        [dot_nt(tp_in()[...], normed), jnp.zeros((8 - NH, T), F32)], axis=0
    )
    segf = seg_in()[...].astype(F32)
    raw_ref[8:16, :] = jnp.broadcast_to(segf, (8, T))
    inner_scr[...] = dot_tt(ip_in()[...], normed)
    inner_ref[...] = inner_scr[...].astype(BF).T
    states = dot_tt(sp_in()[...], normed)
    states_ref[...] = states.astype(BF).T
    gate_ref[...] = dot_tt(gp_in()[...], normed)
    for k in (1, 2, 6, 8, 9, 10, 11):
        targets[k].put()
    cot_ref = cot_in()
    dno_ref[...] = dot_nt(op_in()[...], cot_ref[...])
    cot_part_ref[...] = cot_ref[own, :]
    targets[5].put()
    targets[14].put()

    masks = conv_masks(segf)
    head = head_ref[...]
    step = softplus(raw_ref[0:8, :] + head[:, 8:9])
    rate = -jnp.exp(head[:, 9:10])
    logs, lcols = scan_logs(step, rate, rows_scr, segf)

    spre = conv_forward(
        states, [scols_ref[:, k : k + 1] for k in range(KERNEL)], scols_ref[:, 4:5], masks
    )
    spre_ref[...] = spre
    targets[7].put()
    cs = spre * sigmoid(spre)
    b_tok = cs[0:N, :].T.astype(BF)
    c_low = cs[N:, :].astype(BF)
    for h in range(NH):
        hs = slice(h * HD, (h + 1) * HD)
        pre = conv_forward(
            inner_scr[hs, :], [cols_ref[hs, k : k + 1] for k in range(KERNEL)],
            cols_ref[hs, 4:5], masks,
        )
        pre_ref[hs, :] = pre
        u_scr[hs, :] = pre * sigmoid(pre)
    targets[3].put()
    tail, entry = state_rows(logs, segf)
    weighted = u_scr[:, 0:GROUP] * per_head(step[:, 0:GROUP] * tail, GROUP)
    state = dot(weighted.astype(BF), b_tok[0:GROUP, :])
    entering = dot(state.astype(BF), c_low[:, GROUP:])
    for c in range(2):
        sl = slice(c * GROUP, (c + 1) * GROUP)
        neg = link_mask(lcols, segf, c)
        scores = dot(b_tok[sl, :], c_low[:, sl])
        for h in range(NH):
            hs = slice(h * HD, (h + 1) * HD)
            decay = jnp.exp((logs[h : h + 1, sl] - lcols[sl, h : h + 1]) + neg)
            m = (scores * decay).astype(BF)
            u = u_scr[hs, sl]
            y = dot((u * step[h : h + 1, sl]).astype(BF), m)
            if c == 1:
                y = y + entering[hs, :] * entry[h : h + 1, :]
            mixed_ref[hs, sl] = y + head[h : h + 1, 10:11] * u
    targets[4].put()
    squares = jnp.zeros((1, T), F32)
    dots = jnp.zeros((1, T), F32)
    for h in range(NH):
        hs = slice(h * HD, (h + 1) * HD)
        g = gate_ref[hs, :]
        gated = mixed_ref[hs, :] * (g * sigmoid(g))
        squares = squares + jnp.sum(gated * gated, axis=0, keepdims=True)
        dots = dots + jnp.sum(dno_ref[hs, :] * cols_ref[hs, 5:6] * gated, axis=0, keepdims=True)
    sums_ref[...] = jnp.broadcast_to(
        jnp.concatenate([squares, dots], axis=0)[None], sums_ref.shape
    )


def forward(*args):
    outs = [
        sds((T, D), BF), sds((C, T), F32), sds((T, C), BF), sds((C, T), F32), sds((C, T), F32),
        sds((C, T), F32), sds((T, 256), BF), sds((256, T), F32), sds((16, T), F32),
        sds((C, 8), F32), sds((256, 8), F32), sds((8, 128), F32), sds((8, 2, T), F32),
        sds((64, D), BF), sds((64, D), BF), sds((T, D), BF), sds((T, D), BF),
    ]
    scratch = [
        pltpu.VMEM((128, T), F32), pltpu.VMEM((128, 640), F32), pltpu.VMEM((C, T), F32),
        pltpu.VMEM((C, T), F32),
    ]
    return call(
        fwd_kernel, outs, args, scratch, "forward", near_out=(1, 4, 5, 15, 16), into={16: 16},
        twin={0: 15}, split=0,
    )


def mid_kernel(idx_ref, sources, targets, no_scr, low_scr, out_scr, gate_scr, sems):
    sums_in, gate_in, mixed_in, dno_in, cols_in, cot_in, normed_in = sources
    _, no_ref, gate_low_ref, dy_ref, gain_ref = [t.ref for t in targets]
    grads = targets[0]
    total = jnp.sum(sums_in()[...], axis=0)
    scale = lax.rsqrt(total[0:1, :] / INNER + EPS)
    slope = scale * scale * scale * (total[1:2, :] / INNER)
    gate_ref, mixed_ref, dno_ref, cols_ref = gate_in(), mixed_in(), dno_in(), cols_in()
    for h in range(NH):
        hs = slice(h * HD, (h + 1) * HD)
        g = gate_ref[hs, :]
        s = sigmoid(g)
        silu = g * s
        mixed = mixed_ref[hs, :]
        gated = mixed * silu
        gain = cols_ref[hs, 5:6]
        normal = gated * scale
        no_scr[hs, :] = (normal * gain).astype(BF)
        dno = dno_ref[hs, :]
        gain_ref[hs, :] = jnp.broadcast_to(jnp.sum(dno * normal, axis=1, keepdims=True), (HD, 8))
        d_gated = scale * (dno * gain) - gated * slope
        low_scr[hs, :] = (d_gated * mixed * (s * (1.0 + g * (1.0 - s)))).astype(BF)
        dy_ref[hs, :] = (d_gated * silu).astype(BF)
    targets[3].put()
    out_scr[...] = dot(no_scr[...], cot_in()[...]).astype(BF).reshape(4, 96, D)
    for k in range(4):
        source = out_scr.at[:, :, k * C : (k + 1) * C]
        grads.copies.append(
            pltpu.make_async_copy(source, grads.hbm.at[4 * k : 4 * k + 4, 96:192], sems.at[k])
        )
        grads.copies[-1].start()
    no_ref[...] = no_scr[...].T
    gate_low_ref[...] = low_scr[...].T
    targets[1].put()
    targets[2].put()
    gate_scr[...] = dot(low_scr[...], normed_in()[...]).T.astype(BF).reshape(16, 96, C)
    grads.copies.append(pltpu.make_async_copy(gate_scr, grads.hbm.at[:, 0:96], sems.at[4]))
    grads.copies[-1].start()


def middle(*args):
    outs = [
        sds((16, 192, C), BF), sds((T, C), BF), sds((T, C), BF), sds((C, T), BF), sds((C, 8), F32),
    ]
    scratch = [
        pltpu.VMEM((C, T), BF), pltpu.VMEM((C, T), BF), pltpu.VMEM((4, 96, D), BF),
        pltpu.VMEM((16, 96, C), BF), pltpu.SemaphoreType.DMA((5,)),
    ]
    return call(mid_kernel, outs, args, scratch, "middle", near=(1, 2, 3, 5, 6), free=(0,))


def bwd_kernel(
    idx_ref, sources, targets, rows_scr, u_scr, di_scr, mark_scr, cs_scr, dp_scr, tpad, dps_scr,
    grad_scr, tok_scr, low_tok, step_tok, give_scr, inner_scr,
):
    (
        raw_in, head_in, spre_in, pre_in, dy_in, ic_in, inner_in, normed_in, sc_in,
        states_in, gate_low_in, sp_in, tp_in, gp_in, ip_in, no_in, op_in,
    ) = sources
    _, keep_ref, keep_state_ref, extra_ref, give_state_ref, *gives = [
        t.ref for t in targets
    ]
    core = idx_ref[0]
    raw_ref, head_ref, spre_ref = raw_in(), head_in(), spre_in()
    segf = raw_ref[8:9, :]
    later = [
        ((pltpu.roll(segf, T - k, 1) == segf) & (lane_ids(1, T) < T - k)).astype(F32)
        for k in range(1, KERNEL)
    ]
    head = head_ref[...]
    raw = raw_ref[0:8, :] + head[:, 8:9]
    step = softplus(raw)
    rate = -jnp.exp(head[:, 9:10])
    logs, lcols = scan_logs(step, rate, rows_scr, segf, later)
    marks = [jnp.broadcast_to(lcols[:, 9 + k : 10 + k], (T, 128)) for k in range(3)]
    for k in range(3):
        mark_scr[k] = marks[k]
    spre = spre_ref[...]
    cs = spre * sigmoid(spre)
    b_low = cs[0:N, :].astype(BF)
    c_low = cs[N:, :].astype(BF)
    b_tok = cs[0:N, :].T.astype(BF)
    c_tok = cs[N:, :].T.astype(BF)
    pre_ref, dy_ref = pre_in(), dy_in()
    for h in range(NH):
        hs = slice(h * HD, (h + 1) * HD)
        pre = pre_ref[hs, :]
        u_scr[hs, :] = pre * sigmoid(pre)
    tail, entry = state_rows(logs, segf)
    first, second = slice(0, GROUP), slice(GROUP, T)
    weighted = (u_scr[:, first] * per_head(step[:, first] * tail, GROUP)).astype(BF)
    state = dot(weighted, b_tok[first, :]).astype(BF)
    d_entering = (dy_ref[:, second] * per_head(entry, GROUP)).astype(BF)
    d_state = dot(d_entering, c_tok[second, :]).astype(BF)
    entering = dot(state, c_low[:, second])
    into = dot(d_state, b_low[:, first])
    d_c_second = dot_tn(state, d_entering)
    d_b_first = dot_tn(d_state, weighted)
    tri = (row_ids(GROUP, GROUP) >= lane_ids(GROUP, GROUP)).astype(BF)
    before = (row_ids(GROUP, GROUP) < lane_ids(GROUP, GROUP)).astype(F32)
    upto = (row_ids(GROUP, GROUP) < lane_ids(GROUP, GROUP)).astype(F32)
    since = (row_ids(GROUP, GROUP) >= lane_ids(GROUP, GROUP)).astype(F32)
    out_step = []
    out_skip = []
    da_rows = [[None, None] for _ in range(NH)]
    for c in range(2):
        sl = slice(c * GROUP, (c + 1) * GROUP)
        neg = link_mask(lcols, segf, c)
        scores = dot(b_tok[sl, :], c_low[:, sl])
        d_scores = jnp.zeros((GROUP, GROUP), F32)
        for h in range(NH):
            hs = slice(h * HD, (h + 1) * HD)
            decay = jnp.exp((logs[h : h + 1, sl] - lcols[sl, h : h + 1]) + neg)
            m = scores * decay
            dy = dy_ref[hs, sl]
            inflow = (u_scr[hs, sl] * step[h : h + 1, sl]).astype(BF)
            g = dot_tn(inflow, dy)
            d_scores = d_scores + g * decay
            w = dot((g * m).astype(BF), tri)
            da = jnp.sum(w * before, axis=0, keepdims=True)
            da_rows[h][c] = da
            di = dot_nt(dy, m.astype(BF))
            if c == 0:
                di = di + into[hs, :] * tail[h : h + 1, :]
            di_scr[hs, sl] = di
        ds = d_scores.astype(BF)
        d_b = dot_nt(c_low[:, sl], ds)
        d_c = dot(b_low[:, sl], ds)
        if c == 0:
            d_b = d_b + d_b_first
        else:
            d_c = d_c + d_c_second
        cs_scr[0:N, sl] = d_b
        cs_scr[N:, sl] = d_c
    ic_ref, inner_ref, normed_ref = ic_in(), inner_in(), normed_in()
    zero = jnp.zeros((1, GROUP), F32)
    q_rows, e_rows = [], []
    for h in range(NH):
        hs = slice(h * HD, (h + 1) * HD)
        q = u_scr[hs, first] * step[h : h + 1, first] * into[hs, :]
        q_rows.append(jnp.sum(q, axis=0, keepdims=True))
        e = dy_ref[hs, second] * entering[hs, :]
        e_rows.append(jnp.sum(e, axis=0, keepdims=True))
    q8 = jnp.concatenate(q_rows + [zero, zero], axis=0) * tail
    e8 = jnp.concatenate(e_rows + [zero, zero], axis=0) * entry
    da0 = jnp.concatenate([da_rows[h][0] for h in range(NH)] + [zero, zero], axis=0)
    da1 = jnp.concatenate([da_rows[h][1] for h in range(NH)] + [zero, zero], axis=0)
    da = jnp.concatenate([da0 + dot(q8, upto, EXACT), da1 + dot(e8, since, EXACT)], axis=1)
    d_steps = []
    for h in range(NH):
        hs = slice(h * HD, (h + 1) * HD)
        pre = pre_ref[hs, :]
        s = sigmoid(pre)
        u = u_scr[hs, :]
        di = di_scr[hs, :]
        dy = dy_ref[hs, :].astype(F32)
        d_steps.append(jnp.sum(di * u, axis=0, keepdims=True))
        out_skip.append(jnp.sum(dy * u, axis=0, keepdims=True))
        d_u = di * step[h : h + 1, :] + head[h : h + 1, 10:11] * dy
        d_pre = d_u * (s * (1.0 + pre * (1.0 - s)))
        di_scr[hs, :] = d_pre
    zero = jnp.zeros((2, T), F32)
    d_step = jnp.concatenate(d_steps + [zero], axis=0) + da * rate
    skips = jnp.concatenate(out_skip + [zero], axis=0)
    d_raw = d_step * sigmoid(raw)
    dp_scr[0:T, :] = di_scr[...].T
    dp_scr[T:, :] = jnp.zeros((8, C), F32)
    rows = conv_backward(dp_scr, inner_ref, ic_ref, mark_scr, low_tok)
    inner_grad = dot_tn(normed_ref[...], low_tok[...]).astype(BF)
    inner_scr[...] = inner_grad.reshape(16, 96, C)
    buffer = targets[0]
    buffer.copies.append(pltpu.make_async_copy(inner_scr, buffer.hbm.at[:, 0:96], buffer.sem))
    buffer.copies[-1].start()
    rows_scr[...] = jnp.zeros_like(rows_scr)
    rows_scr[0:8, :] = d_raw
    step_tok[...] = rows_scr[...].T.astype(BF)
    extra_ref[0:8, :] = dot(d_raw.astype(BF), normed_ref[...])
    sc_ref, states_ref = sc_in(), states_in()
    for part in range(4):
        rs = slice(part * 64, (part + 1) * 64)
        pre = spre_ref[rs, :]
        s = sigmoid(pre)
        cs_scr[rs, :] = cs_scr[rs, :] * (s * (1.0 + pre * (1.0 - s)))
    dps_scr[0:T, :] = cs_scr[...].T
    dps_scr[T:, :] = jnp.zeros((8, 256), F32)
    state_rows_ = conv_backward(dps_scr, states_ref, sc_ref, mark_scr, tok_scr)
    columns = [
        jnp.sum(d_raw, axis=1, keepdims=True), jnp.sum(da * step, axis=1, keepdims=True) * rate,
        jnp.sum(skips, axis=1, keepdims=True), jnp.zeros((8, 125), F32),
    ]
    extra_ref[8:16, :] = jnp.concatenate(
        [rows, *columns, jnp.zeros((8, D - C - 128), F32)], axis=1
    )
    targets[3].put()
    taps = jnp.concatenate(
        [
            jnp.concatenate([state_rows_, jnp.zeros((8, D - 256), F32)], axis=1),
            jnp.zeros((8, D), F32),
        ],
        axis=0,
    ).astype(BF)
    grad_scr[...] = dot_tn(tok_scr[...], normed_ref[...]).astype(BF)
    tpad[...] = jnp.zeros_like(tpad)
    tpad[0:NH, :] = tp_in()[...]
    gate_low_ref, no_ref = gate_low_in(), no_in()
    gp_ref, ip_ref, sp_ref, op_ref = gp_in(), ip_in(), sp_in(), op_in()
    for give, half in ((True, 1 - core), (False, core)):
        tok = pl.ds(pl.multiple_of(half * GROUP, GROUP), GROUP)
        total = dot_nt(gate_low_ref[tok, :], gp_ref[...])
        total = total + dot_nt(low_tok[tok, :], ip_ref[...])
        total = total + dot_nt(tok_scr[tok, :], sp_ref[...])
        total = (total + dot(step_tok[tok, :], tpad[...])).astype(BF)
        out = dot(no_ref[tok, :], op_ref[...]).astype(BF)
        for k in range(4):
            slot = lax.rem(k + 4 - idx_ref[1], 4)
            rows = pl.ds(pl.multiple_of(half * 128 + k * 32, 32), 32)
            ref, state_ref = (give_scr, give_state_ref) if give else (keep_ref, keep_state_ref)
            ref[slot, 0:64, :] = total[k * 64 : (k + 1) * 64, :]
            ref[slot, 64:128, :] = out[k * 64 : (k + 1) * 64, :]
            state_ref[slot, 0:32, :] = grad_scr[rows, :]
            state_ref[slot, 32:48, :] = taps
        if give:
            for k in range(4):
                gives[k][...] = give_scr[k]


def backward(*args):
    outs = [
        sds((16, 112, C), BF), sds((4, 128, D), BF), sds((4, 48, D), BF), sds((16, D), F32),
        sds((4, 48, D), BF), *[sds((128, D), BF)] * 4,
    ]
    scratch = [
        pltpu.VMEM((128, T), F32), pltpu.VMEM((C, T), F32), pltpu.VMEM((C, T), F32),
        pltpu.VMEM((3, T, 128), F32), pltpu.VMEM((256, T), F32), pltpu.VMEM((T + 8, C), F32),
        pltpu.VMEM((128, D), BF), pltpu.VMEM((T + 8, 256), F32), pltpu.VMEM((256, D), BF),
        pltpu.VMEM((T, 256), BF), pltpu.VMEM((T, C), BF), pltpu.VMEM((T, 128), BF),
        pltpu.VMEM((4, 128, D), BF), pltpu.VMEM((16, 96, C), BF),
    ]
    return call(
        bwd_kernel, outs, args, scratch, "backward",
        near_out=(1, 2, 4, 5, 6, 7, 8),
    )


def fold_kernel(idx_ref, keep, *refs):
    *got, own_hbm, s1, s2, s3, own, sem = refs

    def both(k):
        other = got[k][...] if len(got) == 4 else got[0][k]
        return keep[k].astype(F32) + other.astype(F32)

    own[...] = both(0)
    store = pltpu.make_async_copy(own, own_hbm, sem)
    store.start()
    for k, send in enumerate((s1, s2, s3)):
        send[...] = both(k + 1).astype(BF)
    store.wait()


def swap(v):
    return lax.ppermute(v, "core", [(0, 1), (1, 0)])


def turn(v, axis, by):
    return lax.ppermute(v, axis, [(i, (i + by) % 4) for i in range(4)])


def fold(idx, keep, got, name):
    rows = keep.shape[1]
    own, *sends = launch(
        fold_kernel, [sds((rows, D), F32), *[sds((rows, D), BF)] * 3], (idx, keep, *got),
        [pltpu.VMEM((rows, D), F32), pltpu.SemaphoreType.DMA(())], name, [NEAR] * (1 + len(got)),
        [FAR] + [NEAR] * 3, vmem=16,
    )
    return [own, *[turn(send, "y", k + 1) for k, send in enumerate(sends)]]


def scatter(idx, keep, keep_state, give_state, gives):
    state = fold(idx, keep_state, [swap(give_state)], "fold_state")
    return state, fold(after(idx, state[0]), keep, [swap(give) for give in gives], "fold")


def spread_out(chunk):
    return [chunk] + [turn(chunk, "y", k) for k in range(1, 4)]


def gather(pieces, *earlier):
    return pieces + [swap(after(piece, *earlier)) for piece in pieces]


def place_of(idx_ref, k):
    half = idx_ref[0] if k < 4 else 1 - idx_ref[0]
    return half, half * 4 + lax.rem(idx_ref[1] + 4 - k % 4, 4)


def finish_kernel(idx_ref, *refs):
    pieces, out_hbm, grad_hbm = refs[:8], refs[8], refs[9]
    buf, grad, in_sems, out_sems = refs[10:]
    loads = [pltpu.make_async_copy(pieces[k], buf.at[k], in_sems.at[k]) for k in range(8)]
    for load in loads:
        load.start()
    stores = []
    for k in range(8):
        _, place = place_of(idx_ref, k)
        rows = pl.ds(pl.multiple_of(place * 64, 64), 64)
        loads[k].wait()
        stores.append(
            pltpu.make_async_copy(buf.at[k, 64:128], out_hbm.at[rows], out_sems.at[0, k])
        )
        stores[-1].start()
        grad[k] = buf[k, 0:64, :].astype(F32)
        stores.append(pltpu.make_async_copy(grad.at[k], grad_hbm.at[rows], out_sems.at[1, k]))
        stores[-1].start()
    for store in stores:
        store.wait()


def ends_kernel(idx_ref, sources, targets, state_scr, small_scr):
    (
        state_ref, norm_ref, sconv_ref, sbias_ref, step_ref, taps_ref, bias_ref, tb_ref, dl_ref,
        sk_ref, gnw_ref,
    ) = [t.ref for t in targets]
    for k in range(8):
        _, place = place_of(idx_ref, k)
        piece = sources[k]()
        for j in range(4):
            columns = slice(j * C, (j + 1) * C)
            for half in range(2):
                rows = pl.ds(pl.multiple_of(place * 32 + half * 16, 16), 16)
                state_scr[rows, columns] = piece[j * 4 + half].astype(F32)
            small_scr[place, :, columns] = piece[j * 4 + 2].astype(F32)
    for row in range(12):
        sl = slice(row * 128, (row + 1) * 128)
        state_ref[sl, :] = state_scr[:, sl].T
    targets[0].put()
    sconv_ref[...] = small_scr[0, 0:4, 0:256]
    sbias_ref[...] = small_scr[0, 4:5, 0:256].reshape(256)
    norm = small_scr[0, 8:9, :]
    for k in range(1, 8):
        norm = norm + small_scr[k, 8:9, :]
    norm_ref[...] = norm.reshape(D)
    own = sources[0]()
    for j in range(4):
        step_ref[:, j * C : (j + 1) * C] = own[j * 4 + 3][0:NH, :].astype(F32)
    smalls = jnp.concatenate([own[3], own[7]], axis=1)[8:16, :].astype(F32)
    taps_ref[...] = smalls[0:4, 0:C]
    bias_ref[...] = smalls[4:5, 0:C].reshape(C)
    gnw_ref[...] = smalls[5:6, 0:C].reshape(C)
    heads = jnp.concatenate([smalls[:, C : C + 128], jnp.zeros((120, 128), F32)], axis=0).T
    tb_ref[...] = heads[0:1, 0:NH].reshape(NH)
    dl_ref[...] = heads[1:2, 0:NH].reshape(NH)
    sk_ref[...] = heads[2:3, 0:NH].reshape(NH)


def pack_kernel(idx_ref, *refs):
    buf_hbm, own_any, p1_any, p2_any, p3_any, extra_hbm, gain_hbm, out_hbm = refs[:8]
    own, parts, extra, gain, pad, blocks, sems = refs[8:]
    loads = [
        pltpu.make_async_copy(source, target, sems.at[k])
        for k, (source, target) in enumerate(
            (
                (own_any, own), (p1_any, parts.at[0]), (p2_any, parts.at[1]),
                (p3_any, parts.at[2]), (extra_hbm, extra), (gain_hbm, gain),
            )
        )
    ]
    for load in loads:
        load.start()
    for load in loads:
        load.wait()
    total = (own[...] + parts[0].astype(F32)) + (parts[1].astype(F32) + parts[2].astype(F32))
    pad[...] = jnp.zeros_like(pad)
    pad[:, 5:6] = gain[:, 0:1]
    gain_row = jnp.concatenate([pad[...].T[0:8, :], jnp.zeros((8, D - C), F32)], axis=1)
    rows = [
        total[0:16, :], total[16:32, :],
        jnp.concatenate([total[32:40, :], jnp.zeros((8, D), F32)], axis=0),
        jnp.concatenate([extra[0:8, :], extra[8:16, :] + gain_row], axis=0),
    ]
    for k in range(16):
        blocks[k] = rows[k % 4][:, k // 4 * C : (k // 4 + 1) * C].astype(BF)
    store = pltpu.make_async_copy(blocks, out_hbm.at[:, 96:112], sems.at[6])
    store.start()
    store.wait()


def input_kernel(idx_ref, sources, targets):
    x_ref, cot_ref, nw_ref = [source() for source in sources[:3]]
    chunk_ref, norm_ref = [t.ref for t in targets]
    p0, p1, p2, p3 = [source() for source in sources[3:]]
    total = (p0[...] + p1[...].astype(F32)) + (p2[...].astype(F32) + p3[...].astype(F32))
    d_normed = total[0:64, :]
    v = x_ref[...].astype(F32)
    scale = lax.rsqrt(jnp.mean(v * v, axis=1, keepdims=True) + EPS)
    weighted = d_normed * nw_ref[...].reshape(1, D)
    grad = scale * weighted - v * (
        scale * scale * scale * jnp.mean(weighted * v, axis=1, keepdims=True)
    )
    chunk_ref[0:64, :] = (cot_ref[...].astype(F32) + grad).astype(BF)
    chunk_ref[64:128, :] = (v + total[64:128, :]).astype(BF)
    targets[0].put()
    norm = jnp.sum(d_normed * v * scale, axis=0, keepdims=True)
    rows = [norm[:, k * C : (k + 1) * C] for k in range(4)]
    norm_ref[...] = jnp.concatenate([*rows, jnp.zeros((12, C), F32)], axis=0).astype(BF)


def share_kernel(idx_ref, sources, targets):
    parts_ref, out_ref = sources[0](), targets[0].ref
    norm = parts_ref[0, 16:32, :].astype(F32)
    for k in range(1, 16):
        norm = norm + parts_ref[k, 16:32, :].astype(F32)
    for k in range(16):
        if k % 4 == 2:
            row = jnp.concatenate(
                [jnp.zeros((8, C), F32), norm[k // 4 : k // 4 + 1, :], jnp.zeros((7, C), F32)],
                axis=0,
            )
            out_ref[k] = (parts_ref[k, 0:16, :].astype(F32) + row).astype(BF)
        else:
            out_ref[k] = parts_ref[k, 0:16, :]


def total_of(parts_ref):
    total = parts_ref[0].astype(F32)
    for k in range(1, 16):
        total = total + parts_ref[k].astype(F32)
    return total.astype(BF)


def reduce_kernel(idx_ref, sources, targets):
    targets[0].ref[...] = total_of(sources[0]())


def spread_kernel(
    idx_ref, terms_any, first_any, norm_any, small_hbm, wide_hbm, terms, first, norm, own, small,
    load_sems, sems,
):
    pairs = [(terms_any.at[4 * k : 4 * k + 4], terms.at[4 * k : 4 * k + 4]) for k in range(4)]
    pairs += [(first_any, first), (norm_any, norm)]
    loads = [
        pltpu.make_async_copy(source, target, load_sems.at[k])
        for k, (source, target) in enumerate(pairs)
    ]
    for load in loads:
        load.start()
    total = jnp.zeros((112, C), F32)
    for k in range(4):
        loads[k].wait()
        part = terms[4 * k].astype(F32)
        for j in range(1, 4):
            part = part + terms[4 * k + j].astype(F32)
        total = total + part
    own[...] = total.astype(BF)
    loads[4].wait()
    stores = [
        pltpu.make_async_copy(own.at[0:96], wide_hbm.at[k, 192:288], sems.at[k])
        for k in range(4)
    ]
    stores += [
        pltpu.make_async_copy(first, wide_hbm.at[k, 0:192], sems.at[4 + k]) for k in range(4)
    ]
    for store in stores:
        store.start()
    loads[5].wait()
    both = jnp.concatenate([own[96:112, :], norm[...]], axis=0)
    for k in range(16):
        small[k] = both
    stores.append(pltpu.make_async_copy(small, small_hbm, sems.at[8]))
    stores[-1].start()
    for store in stores:
        store.wait()


def again_kernel(idx_ref, blocks_any, out_hbm, blocks, load_sem, sems):
    load = pltpu.make_async_copy(blocks_any, blocks, load_sem)
    load.start()
    load.wait()
    stores = [pltpu.make_async_copy(blocks, out_hbm.at[k], sems.at[k]) for k in range(4)]
    for store in stores:
        store.start()
    for store in stores:
        store.wait()


def widen_kernel(
    idx_ref, hbm, gate_hbm, out_hbm, inner_hbm, buf, gate, out, inner, in_sems, out_sems
):
    loads = [pltpu.make_async_copy(hbm.at[k], buf.at[k], in_sems.at[k]) for k in range(4)]
    for load in loads:
        load.start()
    stores = []
    for k in range(4):
        loads[k].wait()
        for j in range(4):
            gate[k, j] = buf[k, j, 0:96, :].astype(F32)
            out[k, j * 96 : (j + 1) * 96, :] = buf[k, j, 96:192, :].astype(F32)
            inner[k, j] = buf[k, j, 192:288, :].astype(F32)
        columns = slice(k * C, (k + 1) * C)
        for j, (source, target) in enumerate(
            (
                (gate.at[k], gate_hbm.at[k]), (out.at[k], out_hbm.at[:, columns]),
                (inner.at[k], inner_hbm.at[k]),
            )
        ):
            stores.append(pltpu.make_async_copy(source, target, out_sems.at[j, k]))
            stores[-1].start()
    for store in stores:
        store.wait()


def flat(z, x, y, core):
    return ((z * 4 + x) * 4 + y) * 2 + core


def teams(kind):
    out = []
    for core in range(2):
        for y in range(4):
            grid = [
                [flat(b, a, y, 0) if core == 0 else flat(a, b, y, 1) for b in range(4)]
                for a in range(4)
            ]
            if kind == "both":
                out.append([place for row in grid for place in row])
            elif kind == "second":
                out.extend(grid)
            else:
                out.extend([list(column) for column in zip(*grid)])
    return out


def exchange(v, kind):
    return lax.all_to_all(
        v, ("z", "x", "y", "core"), 0, 0, axis_index_groups=teams(kind), tiled=True
    )


def after(idx, *values):
    return lax.optimization_barrier((idx, *values))[0]


def per_device(
    inputs, norm_weight, gate_proj, inner_proj, state_proj, step_proj, inner_conv,
    inner_conv_bias, state_conv, state_conv_bias, step_bias, decay_log, skip_weight,
    gated_norm_weight, out_proj, segments, cotangent,
):
    x, cot, step_rows = inputs[0], cotangent[0], step_proj.T
    dma = pltpu.SemaphoreType.DMA
    idx = jnp.stack([lax.axis_index(a) for a in ("core", "y", "x", "z")]).astype(jnp.int32)
    (
        normed, gate, inner, pre, mixed, dno, states, spre, raw, cols, scols, head, sums, x_part,
        cot_part, normed_here, cot_here,
    ) = forward(
        idx, x, norm_weight, inner_conv, inner_conv_bias, state_conv, state_conv_bias, step_bias,
        decay_log, skip_weight, gated_norm_weight, segments, step_rows, inner_proj, state_proj,
        gate_proj, out_proj, cot,
    )
    sums = lax.all_to_all(sums, ("y", "core"), 0, 0, tiled=True)
    grads, no, gate_low, dy, gain = middle(
        idx, sums, gate, mixed, dno, cols, cot_here, normed_here
    )

    first_terms = exchange(grads, "both")
    inner_grad, keep, keep_state, extra, give_state, *gives = backward(
        idx, raw, head, spre, pre, dy, inner_conv, inner, normed, state_conv, states, gate_low, state_proj,
        step_rows, gate_proj, inner_proj, no, out_proj,
    )
    state_pieces, pieces = scatter(idx, keep, keep_state, give_state, gives)
    (terms,) = launch(
        pack_kernel, [sds((16, 112, C), BF)], (idx, inner_grad, *state_pieces, extra, gain),
        [
            pltpu.VMEM((48, D), F32), pltpu.VMEM((3, 48, D), BF), pltpu.VMEM((16, D), F32),
            pltpu.VMEM((C, 8), F32), pltpu.VMEM((C, 128), F32), pltpu.VMEM((16, 16, C), BF),
            dma((7,)),
        ],
        "pack", [FAR, FAR, FREE, FREE, FREE, FAR, FAR], [FAR], aliases={1: 0},
    )
    second_terms = exchange(terms, "both")
    (first,) = call(
        reduce_kernel, [sds((192, C), BF)], (idx, first_terms), name="reduce", free=(0,),
    )
    chunk, norm = call(
        input_kernel, [sds((128, D), BF), sds((16, C), BF)],
        (idx, x_part, cot_part, norm_weight, *pieces), (), "input_part", free=(4, 5, 6),
        free_out=(0,), us=INPUT_US,
    )
    small, wide = launch(
        spread_kernel, [sds((16, 32, C), BF), sds((4, 288, C), BF)],
        (idx, second_terms, first, norm),
        [
            pltpu.VMEM((16, 112, C), BF), pltpu.VMEM((192, C), BF), pltpu.VMEM((16, C), BF),
            pltpu.VMEM((112, C), BF), pltpu.VMEM((16, 32, C), BF), dma((6,)), dma((9,)),
        ],
        "spread", [FREE, FAR, FAR], [FAR] * 2, SPREAD_US,
    )
    small = exchange(small, "both")
    chunks = spread_out(chunk)
    wide = exchange(after(wide, small, *chunks[1:]), "second")
    (pack,) = call(
        share_kernel, [sds((16, 16, C), BF)], (idx, small), name="share", free=(0,),
        free_out=(0,),
    )
    (wide,) = launch(
        again_kernel, [sds((4, 4, 288, C), BF)], (idx, wide),
        [pltpu.VMEM((4, 288, C), BF), dma(()), dma((4,))], "again", [FREE], [FAR],
    )
    parts = gather(chunks, wide)
    ends = gather(spread_out(pack), wide)
    outputs, input_grad = launch(
        finish_kernel, [sds((T, D), BF), sds((T, D), F32)], (idx, *parts),
        [
            pltpu.VMEM((8, 128, D), BF), pltpu.VMEM((8, 64, D), F32), dma((8,)), dma((2, 8)),
        ],
        "finish", [FREE] * 8, [FAR] * 2, FINISH_US,
    )
    wide = exchange(wide, "first")
    (
        state_grad, norm_grad, sconv, sbias, step_grad, taps, bias, tb, dl, sk, gnw,
    ) = call(
        ends_kernel,
        [
            sds((D, 256), F32), sds((D,), F32), sds((KERNEL, 256), F32), sds((256,), F32),
            sds((NH, D), F32), sds((KERNEL, C), F32), sds((C,), F32), sds((NH,), F32),
            sds((NH,), F32), sds((NH,), F32), sds((C,), F32),
        ],
        (idx, *ends), [pltpu.VMEM((256, D), F32), pltpu.VMEM((8, 16, D), F32)], "ends",
        free=range(8),
    )
    gate_grad, out_grad, inner_grad = launch(
        widen_kernel,
        [sds((4, 4, 96, C), F32), sds((C, D), F32), sds((4, 4, 96, C), F32)], (idx, wide),
        [
            pltpu.VMEM((4, 4, 288, C), BF), pltpu.VMEM((4, 4, 96, C), F32),
            pltpu.VMEM((4, C, C), F32), pltpu.VMEM((4, 4, 96, C), F32), dma((4,)), dma((3, 4)),
        ],
        "widen", [FREE], [FAR] * 3, WIDEN_US,
    )
    return (
        outputs[None], input_grad[None], norm_grad, gate_grad.reshape(D, C),
        inner_grad.reshape(D, C), state_grad, step_grad.T, taps, bias, sconv, sbias, tb, dl, sk,
        gnw, out_grad,
    )


def solution(mesh):
    small = Mesh(mesh.devices.reshape(4, 4, 4, 2), ("z", "x", "y", "core"))
    dp, tp = ("z", "x"), ("y", "core")
    placed = (
        P(dp, None, None), P(), P(None, tp), P(None, tp), P(), P(None, tp), P(None, tp), P(tp),
        P(), P(), P(tp), P(tp), P(tp), P(tp), P(tp, None), P(dp, None), P(dp, None, None),
    )
    out = (
        P(dp, None, None), P(dp, None, None), P(), P(None, tp), P(None, tp), P(), P(None, tp),
        P(None, tp), P(tp), P(), P(), P(tp), P(tp), P(tp), P(tp), P(tp, None),
    )
    return jax.shard_map(per_device, mesh=small, in_specs=placed, out_specs=out, check_vma=False)
```
